32 devices in a mesh: tok: 8 (over z, y), head: 4 (over x, core).
Axes of the slice: x: 2, y: 2, z: 4, core: 2. Of those that a mesh axis runs over, the one named last changes fastest.
Arguments:
- queries: bfloat16 [2048, 24, 128], P('tok', 'head'), may hold values from -4.5 to 4.5
- keys: bfloat16 [2048, 24, 128], P('tok', 'head'), may hold values from -4.5 to 4.5
- values: bfloat16 [2048, 24, 128], P('tok', 'head'), may hold values from -5 to 5
- grad_out: bfloat16 [2048, 3072], P('tok', 'head'), may hold values from -6 to 6
- w_out: bfloat16 [3072, 3072], P('head'), may hold values from -0.109375 to 0.109375
- crit: int32 [8, 40], P('tok'), may hold values from -1 to 127, as said below
Outputs:
- grad_q: bfloat16 [2048, 24, 128], P('tok', 'head')
- grad_k: bfloat16 [2048, 24, 128], P('tok', 'head')
- grad_v: bfloat16 [2048, 24, 128], P('tok', 'head')
The draws below stay inside these ranges and needn't reach their ends.
Inputs may be any that keep to these rules, and one draw needn't show every extreme that they name: `crit`: row b lists distinct key tiles, -1 marking unused entries, which come last; no listed tile lies in query block b - 1, b or b + 1 (not counted round); at most 8 tiles of one row lie in one query block, and some row has 8 tiles in one block; row 0 lists a tile of block 7 and row 7 a tile of block 0; some row has no unused entry, and every row uses half of its entries or more.
All inputs are finite; a program needn't handle non-finite values.
Results may differ from the reference program's by a relative error of at most 0.022.
Values may be sent and summed in bfloat16 or wider, within the bound.
A program may use at most 128 MiB of HBM per device.

```python
import jax
import jax.numpy as jnp
from jax import lax

D = 3072
HEADS = 24
HDIM = 128
TOK_DEV = 256
KT = 16
NCRIT = 40
TOKENS = 2048


def draw_queries(key, part):
    key = jax.random.fold_in(key, 3)
    shape = (TOKENS, HEADS, HDIM)
    base = jnp.clip(jax.random.normal(key, shape, jnp.float32), -4.5, 4.5)
    return base.astype(jnp.bfloat16)


def draw_keys(key, part):
    key = jax.random.fold_in(key, 5)
    shape = (TOKENS, HEADS, HDIM)
    base = jnp.clip(jax.random.normal(key, shape, jnp.float32), -4.5, 4.5)
    return base.astype(jnp.bfloat16)


def draw_crit(key, part):
    key = jax.random.fold_in(key, 11)
    blocks = TOKENS // TOK_DEV
    per_block = TOK_DEV // KT
    far = blocks - 3
    capacity = (NCRIT + blocks - 4) // (blocks - 3)
    keys_a, key_b, keys_c, key_d, key_e = jax.random.split(key, 5)
    owner_perm = jax.vmap(lambda sub: jax.random.permutation(sub, far))(jax.random.split(keys_a, blocks))
    entry = jnp.arange(NCRIT)
    rank = entry // capacity
    slot = entry % capacity
    block_ids = jnp.arange(blocks)
    owner = (block_ids[:, None] + owner_perm[:, rank] + 2) % blocks
    first_rank = (rank == 0)[None, :]
    owner = jnp.where(first_rank & (block_ids[:, None] == 0), blocks - 1, owner)
    owner = jnp.where(first_rank & (block_ids[:, None] == blocks - 1), 0, owner)
    start = jax.random.randint(key_b, (blocks, far), 0, per_block)[:, rank]
    tiles = owner * per_block + (start + slot[None, :]) % per_block
    order = jax.vmap(lambda sub: jax.random.permutation(sub, NCRIT))(jax.random.split(keys_c, blocks))
    tiles = jnp.take_along_axis(tiles, order, axis=1)
    lengths = jax.random.randint(key_d, (blocks,), NCRIT // 2, NCRIT + 1)
    full_row = jax.random.randint(key_e, (), 0, blocks)
    lengths = jnp.where(block_ids == full_row, NCRIT, lengths)
    lengths = jnp.where((block_ids == 0) | (block_ids == blocks - 1), NCRIT, lengths)
    return jnp.where(entry[None, :] < lengths[:, None], tiles, -1).astype(jnp.int32)


def shard_levels(stream_key, shape, pieces, smallest, top_value):
    def one(axis_at, shards_of):
        heights = jax.random.uniform(jax.random.fold_in(jax.random.fold_in(stream_key, 6), axis_at), (shards_of,), jnp.float32, smallest / len(pieces), top_value / len(pieces))
        return jnp.repeat(jnp.exp(heights), shape[axis_at] // shards_of).reshape((-1,) + (1,) * (len(shape) - axis_at - 1))

    level = one(*pieces[0])
    for cut in pieces[1:]:
        level = level * one(*cut)
    return level


def centred(stream_key, shape, deviation, limit, cuts=(), held_as=jnp.bfloat16):
    result = jax.random.normal(stream_key, shape, jnp.float32) * deviation
    if len(cuts) > 0:
        result = shard_levels(stream_key, shape, cuts, -0.22, 0.18) * result
    return jnp.clip(result, min=-limit, max=limit).astype(held_as)


def setup_inputs(seed: int = 0) -> dict:
    splits = jax.random.split(jax.random.key(seed), 7)
    return {
        "queries": draw_queries(jax.random.fold_in(splits[6], 71), 0),
        "keys": draw_keys(jax.random.fold_in(splits[6], 71), 0),
        "values": centred(splits[2], (TOKENS, HEADS, HDIM), 1.0, 5.0, ((0, 8), (1, 4))),
        "grad_out": centred(splits[3], (TOKENS, D), 1.0, 6.0, ((0, 8), (1, 4))),
        "w_out": centred(splits[4], (D, D), D ** -0.5, 0.109375, ((0, 4),)),
        "crit": draw_crit(jax.random.fold_in(splits[6], 71), 0),
    }


def reference(queries, keys, values, grad_out, w_out, crit):
    d_attn = jnp.dot(grad_out, w_out.T, preferred_element_type=jnp.float32).astype(jnp.bfloat16)
    d_attn = d_attn.reshape(TOKENS, HEADS, HDIM)
    blocks = TOKENS // TOK_DEV
    scale = HDIM ** -0.5
    tile_off = jnp.arange(KT, dtype=jnp.int32)

    def step(carry, b):
        acc_k, acc_v = carry
        start = b * TOK_DEV
        own_idx = start + jnp.arange(TOK_DEV, dtype=jnp.int32)
        left_idx = start - KT + tile_off
        right_idx = start + TOK_DEV + tile_off
        tiles = lax.dynamic_index_in_dim(crit, b, 0, keepdims=False)
        far_idx = (tiles[:, None] * KT + tile_off[None, :]).reshape(-1)
        index = jnp.concatenate([left_idx, own_idx, right_idx, far_idx]).astype(jnp.int32)
        valid = jnp.concatenate([jnp.broadcast_to(b > 0, (KT,)), jnp.ones((TOK_DEV,), bool),
                                 jnp.broadcast_to(b < blocks - 1, (KT,)), jnp.repeat(tiles >= 0, KT)])
        safe = jnp.clip(index, 0, TOKENS - 1).astype(jnp.int32)
        query = lax.dynamic_slice_in_dim(queries, start, TOK_DEV, 0).astype(jnp.float32)
        grad_o = lax.dynamic_slice_in_dim(d_attn, start, TOK_DEV, 0).astype(jnp.float32)
        key_b = jnp.take(keys, safe, axis=0).astype(jnp.float32)
        val_b = jnp.take(values, safe, axis=0).astype(jnp.float32)
        scores = jnp.einsum("qhd,khd->hqk", query, key_b) * scale
        scores = jnp.where(valid[None, None, :], scores, -1e30)
        top = jnp.max(scores, axis=-1, keepdims=True)
        probs = jnp.exp(scores - top)
        probs = probs / jnp.sum(probs, axis=-1, keepdims=True)
        probs_b = probs.astype(jnp.bfloat16)
        dprob = jnp.einsum("qhd,khd->hqk", grad_o, val_b)
        delta = jnp.sum(probs * dprob, axis=-1, keepdims=True)
        dscore = (probs * (dprob - delta) * scale).astype(jnp.bfloat16)
        grad_q = jnp.einsum("hqk,khd->qhd", dscore.astype(jnp.float32), key_b).astype(jnp.bfloat16)
        weight = valid.astype(jnp.float32)[:, None, None]
        part_k = jnp.einsum("hqk,qhd->khd", dscore.astype(jnp.float32), query) * weight
        part_v = jnp.einsum("hqk,qhd->khd", probs_b.astype(jnp.float32), grad_o) * weight
        acc_k = acc_k.at[safe].add(part_k)
        acc_v = acc_v.at[safe].add(part_v)
        return (acc_k, acc_v), grad_q

    zeros = jnp.zeros((TOKENS, HEADS, HDIM), jnp.float32)
    (acc_k, acc_v), grad_qs = lax.scan(step, (zeros, zeros), jnp.arange(blocks, dtype=jnp.int32))
    return grad_qs.reshape(TOKENS, HEADS, HDIM), acc_k.astype(jnp.bfloat16), acc_v.astype(jnp.bfloat16)
```

```python
import functools

import jax
import jax.numpy as jnp
from jax import lax
from jax.experimental import pallas as pl
from jax.experimental.pallas import tpu as pltpu
from jax.sharding import PartitionSpec as P

KT = 16
LANES = 128
MASKED = -1e30
MESH = pl.DeviceIdType.MESH
NT = (((1,), (1,)), ((), ()))


def owner_of(h, group, count, heads):
    gap = count - heads
    odd = group % 2
    late = jnp.where(h >= heads // 2, gap, 0)
    return h + jnp.where(odd == 1, late, gap // 2)


def head_of(me, group, count, heads):
    gap = count - heads
    half = heads // 2
    odd = group % 2
    even_head = me - gap // 2
    odd_head = jnp.where(me < half, me, me - gap)
    even_owns = (even_head >= 0) & (even_head < heads)
    odd_owns = (me < half) | (me >= half + gap)
    owns = ((odd == 1) & odd_owns) | ((odd == 0) & even_owns)
    head = jnp.where(odd == 1, odd_head, even_head)
    return jnp.clip(head, 0, heads - 1), owns


def by_head_kernel(
    count, groups, ncrit, crit, q_in, k_in, v_in, go_in, w_in, dq_out, dk_out, dv_out,
    q_all, k_all, v_all, d_all, bias_own, bias_all, go_all, w_all, acc, d_own, onehot, k_turned,
    weights, scores, dprob, inverse, dk_acc, dv_acc, dq_st, dk_st, dv_st,
    send_in, recv_in, send_go, recv_go, w_sem, send_out, recv_out,
):
    heads, rows, dim = q_in.shape
    total = count * rows
    tiles_here = rows // KT
    width = go_in.shape[1]
    me = lax.axis_index("tok")
    group = lax.axis_index("head")
    head, owns = head_of(me, group, count, heads)

    barrier = pltpu.get_barrier_semaphore()
    for step in range(1, count):
        pl.semaphore_signal(
            barrier, inc=1, device_id=((me + step) % count, group), device_id_type=MESH
        )
    for step in range(1, groups):
        pl.semaphore_signal(
            barrier, inc=1, device_id=(me, (group + step) % groups), device_id_type=MESH
        )
    loads = []
    for s in range(groups):
        load = pltpu.make_async_copy(w_in.at[:, pl.ds(s * width, width)], w_all.at[s], w_sem.at[s])
        load.start()
        loads.append(load)
    tile_ids = lax.broadcasted_iota(jnp.int32, (KT, LANES), 1)
    first = me * tiles_here - 1
    allowed = (tile_ids >= first) & (tile_ids <= first + tiles_here + 1)
    for c in range(ncrit):
        allowed = allowed | (tile_ids == crit[0, c])
    bias_own[...] = jnp.where(allowed, 0.0, MASKED).astype(jnp.bfloat16)
    pl.semaphore_wait(barrier, count - 1 + groups - 1)

    def go_copy(step):
        return pltpu.make_async_remote_copy(
            src_ref=go_in,
            dst_ref=go_all.at[group],
            send_sem=send_go.at[step],
            recv_sem=recv_go.at[step],
            device_id=(me, (group + step) % groups),
            device_id_type=MESH,
        )

    for step in range(1, groups):
        go_copy(step).start()
    own_go = pltpu.make_async_copy(go_in, go_all.at[group], recv_go.at[0])
    own_go.start()

    here = pl.ds(pl.multiple_of(me * rows, rows), rows)

    def target(i):
        half = heads // 2
        far = jnp.where(me < count // 2, half, 0)
        h = (far + (i % half + me) % half + (i // half) * half) % heads
        return h, owner_of(h, group, count, heads)

    def in_copy(kind, src, dst, h, owner):
        return pltpu.make_async_remote_copy(
            src_ref=src,
            dst_ref=dst,
            send_sem=send_in.at[kind, h],
            recv_sem=recv_in.at[kind, me],
            device_id=(owner, group),
            device_id_type=MESH,
        )

    def send(kind, src, dst, h, owner):
        @pl.when(owner != me)
        def _():
            in_copy(kind, src, dst, h, owner).start()

        @pl.when(owner == me)
        def _():
            pltpu.make_async_copy(src, dst, recv_in.at[kind, me]).start()

    for i in range(heads):
        h, owner = target(i)
        send(4, bias_own, bias_all.at[me], h, owner)
        send(0, k_in.at[h], k_all.at[here], h, owner)
    for i in range(heads):
        h, owner = target(i)
        send(1, q_in.at[h], q_all.at[here], h, owner)
    for i in range(heads):
        h, owner = target(i)
        send(2, v_in.at[h], v_all.at[here], h, owner)

    for step in range(groups):
        src = (group + groups - step) % groups
        if step == 0:
            own_go.wait()
        else:
            go_copy(step).wait_recv()
        if step == 0:
            for load in loads:
                load.wait()
        part = lax.dot_general(
            go_all[src], w_all[src], NT, preferred_element_type=jnp.float32
        )
        if step == 0:
            acc[...] = part
        elif step < groups - 1:
            acc[...] += part
        else:
            done = (acc[...] + part).astype(jnp.bfloat16)
            for h in range(heads):
                d_own[h] = done[:, h * dim : (h + 1) * dim]
    for i in range(heads):
        h, owner = target(i)
        send(3, d_own.at[h], d_all.at[here], h, owner)

    def landed(kind, dst, b):
        in_copy_from = pltpu.make_async_remote_copy(
            src_ref=dst,
            dst_ref=dst,
            send_sem=send_in.at[kind, 0],
            recv_sem=recv_in.at[kind, b],
            device_id=((me + 1) % count, group),
            device_id_type=MESH,
        )
        in_copy_from.wait_recv()

    def block(b):
        return pl.ds(pl.multiple_of(b * rows, rows), rows)

    scale = dim ** (-0.5)

    @pl.when(owns)
    def _():
        def prepare(b, carry):
            landed(4, bias_all.at[b], b)
            landed(0, k_all.at[block(b)], b)
            ids = lax.broadcasted_iota(jnp.int32, (rows, LANES), 1)
            of_row = b * tiles_here + lax.broadcasted_iota(jnp.int32, (rows, LANES), 0) // KT
            onehot[block(b), :] = jnp.where(ids == of_row, 1.0, 0.0).astype(jnp.bfloat16)
            k_turned[b] = k_all[block(b), :].T
            return carry

        lax.fori_loop(0, count, prepare, 0)

        def forward(b, carry):
            landed(1, q_all.at[block(b)], b)
            bias = jnp.broadcast_to(bias_all[b][0:1, :], (rows, LANES))
            query = jnp.concatenate([q_all[block(b), :], bias], axis=1)
            top = jnp.full((8, rows), MASKED, jnp.float32)
            for j in range(count):
                at = slice(j * rows, (j + 1) * rows)
                key = jnp.concatenate([k_all[at, :], onehot[at, :]], axis=1)
                s = lax.dot_general(key, query, NT, preferred_element_type=jnp.float32)
                scores[at, :] = s
                top = jnp.maximum(top, jnp.max(s.reshape(rows // 8, 8, rows), axis=0))
            top = jnp.max(top, axis=0, keepdims=True)
            factor = scale * 1.4426950408889634
            summed = jnp.zeros((8, rows), jnp.float32)
            for j in range(count):
                at = slice(j * rows, (j + 1) * rows)
                e = jnp.exp2((scores[at, :] - top) * factor)
                weights[b, at, :] = e.astype(jnp.bfloat16)
                summed = summed + jnp.sum(e.reshape(rows // 8, 8, rows), axis=0)
            inv = 1.0 / jnp.sum(summed, axis=0, keepdims=True)
            inverse[b] = jnp.broadcast_to(inv, (8, rows))
            return carry

        lax.fori_loop(0, count, forward, 0)
        dk_acc[...] = jnp.zeros_like(dk_acc)
        dv_acc[...] = jnp.zeros_like(dv_acc)

        def values_in(b, carry):
            landed(2, v_all.at[block(b)], b)
            return carry

        lax.fori_loop(0, count, values_in, 0)

        def backward(b, carry):
            landed(3, d_all.at[block(b)], b)
            d_b = d_all[block(b), :]
            q_b = q_all[block(b), :]
            inv = inverse[b][0:1, :]
            delta = jnp.zeros((8, rows), jnp.float32)
            for j in range(count):
                at = slice(j * rows, (j + 1) * rows)
                dp = lax.dot_general(v_all[at, :], d_b, NT, preferred_element_type=jnp.float32)
                dprob[at, :] = dp
                w = weights[b, at, :].astype(jnp.float32) * dp
                delta = delta + jnp.sum(w.reshape(rows // 8, 8, rows), axis=0)
            delta = jnp.sum(delta, axis=0, keepdims=True) * inv
            dq = jnp.zeros((dim, rows), jnp.float32)
            for j in range(count):
                at = slice(j * rows, (j + 1) * rows)
                p = weights[b, at, :].astype(jnp.float32) * inv
                ds = (p * (dprob[at, :] - delta)).astype(jnp.bfloat16)
                dv_acc[at, :] += jnp.dot(
                    p.astype(jnp.bfloat16), d_b, preferred_element_type=jnp.float32
                )
                dk_acc[at, :] += jnp.dot(ds, q_b, preferred_element_type=jnp.float32)
                dq = dq + jnp.dot(k_turned[j], ds, preferred_element_type=jnp.float32)
            dq_st[block(b), :] = (dq * scale).T.astype(jnp.bfloat16)
            give(0, dq_st, dq_out, b)
            return carry

        def out_copy(kind, staged, out, b):
            return pltpu.make_async_remote_copy(
                src_ref=staged.at[block(b)],
                dst_ref=out.at[head],
                send_sem=send_out.at[kind, b],
                recv_sem=recv_out.at[kind, head],
                device_id=(b, group),
                device_id_type=MESH,
            )

        def give(kind, staged, out, b):
            @pl.when(b != me)
            def _():
                out_copy(kind, staged, out, b).start()

            @pl.when(b == me)
            def _():
                pltpu.make_async_copy(
                    staged.at[block(b)], out.at[head], recv_out.at[kind, head]
                ).start()

        lax.fori_loop(0, count, backward, 0)

        def finish(i, carry):
            b = (me + count // 2 + i) % count
            dk_st[block(b), :] = (dk_acc[block(b), :] * scale).astype(jnp.bfloat16)
            give(1, dk_st, dk_out, b)
            dv_st[block(b), :] = dv_acc[block(b), :].astype(jnp.bfloat16)
            give(2, dv_st, dv_out, b)
            return carry

        lax.fori_loop(0, count, finish, 0)

        def sent(b, carry):
            @pl.when(b != me)
            def _():
                for kind, staged, out in ((0, dq_st, dq_out), (1, dk_st, dk_out), (2, dv_st, dv_out)):
                    out_copy(kind, staged, out, b).wait_send()

            return carry

        lax.fori_loop(0, count, sent, 0)

    for step in range(1, groups):
        go_copy(step).wait_send()
    for h in range(heads):
        owner = owner_of(h, group, count, heads)

        @pl.when(owner != me)
        def _():
            in_copy(0, k_in.at[h], k_all.at[here], h, owner).wait_send()
            in_copy(1, q_in.at[h], q_all.at[here], h, owner).wait_send()
            in_copy(2, v_in.at[h], v_all.at[here], h, owner).wait_send()
            in_copy(3, d_own.at[h], d_all.at[here], h, owner).wait_send()
            in_copy(4, bias_own, bias_all.at[me], h, owner).wait_send()

        for kind, out in ((0, dq_out), (1, dk_out), (2, dv_out)):
            pltpu.make_async_remote_copy(
                src_ref=out.at[h],
                dst_ref=out.at[h],
                send_sem=send_out.at[kind, 0],
                recv_sem=recv_out.at[kind, h],
                device_id=((me + 1) % count, group),
                device_id_type=MESH,
            ).wait_recv()


def by_head(queries, keys, values, grad_out, w_out, crit):
    rows, heads, dim = queries.shape
    count = lax.axis_size("tok")
    groups = lax.axis_size("head")
    total = count * rows
    width = grad_out.shape[1]
    bf16, f32 = jnp.bfloat16, jnp.float32
    anywhere = pl.BlockSpec(memory_space=pl.ANY)
    vmem, dma = pltpu.VMEM, pltpu.SemaphoreType.DMA
    out = jax.ShapeDtypeStruct((heads, rows, dim), bf16)
    grads = pl.pallas_call(
        functools.partial(by_head_kernel, count, groups, crit.shape[1]),
        out_shape=(out, out, out),
        in_specs=[pl.BlockSpec(memory_space=pltpu.SMEM)] + [anywhere] * 5,
        out_specs=(anywhere, anywhere, anywhere),
        scratch_shapes=[
            vmem((total, dim), bf16),
            vmem((total, dim), bf16),
            vmem((total, dim), bf16),
            vmem((total, dim), bf16),
            vmem((KT, LANES), bf16),
            vmem((count, KT, LANES), bf16),
            vmem((groups, rows, width), bf16),
            vmem((groups, w_out.shape[0], width), bf16),
            vmem((rows, heads * dim), f32),
            vmem((heads, rows, dim), bf16),
            vmem((total, LANES), bf16),
            vmem((count, dim, rows), bf16),
            vmem((count, total, rows), bf16),
            vmem((total, rows), f32),
            vmem((total, rows), f32),
            vmem((count, 8, rows), f32),
            vmem((total, dim), f32),
            vmem((total, dim), f32),
            vmem((total, dim), bf16),
            vmem((total, dim), bf16),
            vmem((total, dim), bf16),
            dma((5, heads)),
            dma((5, count)),
            dma((groups,)),
            dma((groups,)),
            dma((groups,)),
            dma((3, count)),
            dma((3, heads)),
        ],
        compiler_params=pltpu.CompilerParams(
            collective_id=0, has_side_effects=True, vmem_limit_bytes=52 * 2**20
        ),
    )(
        crit,
        jnp.transpose(queries, (1, 0, 2)),
        jnp.transpose(keys, (1, 0, 2)),
        jnp.transpose(values, (1, 0, 2)),
        grad_out,
        w_out,
    )
    return tuple(jnp.transpose(grad, (1, 0, 2)) for grad in grads)


def padded(cells, sides, width):
    for axis, dim in sides:
        count = lax.axis_size(axis)
        ends = count - 1
        head = lax.slice_in_dim(cells, 0, width, axis=dim)
        tail = lax.slice_in_dim(cells, cells.shape[dim] - width, cells.shape[dim], axis=dim)
        cells = jnp.concatenate(
            [
                lax.ppermute(tail, axis, [(i, (i + 1) % count) for i in range(ends)]),
                cells,
                lax.ppermute(head, axis, [((i + 1) % count, i) for i in range(ends)]),
            ],
            axis=dim,
        )
    return cells


def shifted(value, axis, steps):
    count = lax.axis_size(axis)
    leading, last = (max(0, -steps), min(count, count - steps))
    return lax.ppermute(value, axis, [(source, source + steps) for source in range(leading, last)])


def shards(queries, keys, values, grad_out, w_out, crit):
    tok_rows, heads_here, head_dim = queries.shape
    width_here = heads_here * head_dim
    count = lax.axis_size("tok")
    place = lax.axis_index("tok")
    tiles_here = tok_rows // KT
    if heads_here <= count <= 2 * heads_here and count * tiles_here <= LANES:
        return by_head(queries, keys, values, grad_out, w_out, crit)
    ncrit = crit.shape[1]
    capacity = (ncrit + count - 4) // (count - 3)
    slots = count * capacity
    row_len = KT * width_here
    d_attn = lax.dot_general(
        lax.all_gather(grad_out, "head", axis=1, tiled=True),
        w_out,
        (((1,), (1,)), ((), ())),
        preferred_element_type=jnp.float32,
    )
    d_attn = d_attn.astype(jnp.bfloat16).reshape(tok_rows, heads_here, head_dim)
    tiles = crit[0]
    used = tiles >= 0
    owner = jnp.where(used, tiles // tiles_here, -1)
    local_tile = jnp.where(used, tiles % tiles_here, 0)
    order = jnp.arange(ncrit)
    earlier = (owner[:, None] == owner[None, :]) & (order[:, None] > order[None, :]) & used[None, :]
    slot = jnp.sum(earlier.astype(jnp.int32), axis=1)
    position = jnp.where(used, owner * capacity + slot, 0)
    slot_ids = jnp.arange(slots)
    chosen = used[:, None] & (position[:, None] == slot_ids[None, :])
    request = jnp.sum(jnp.where(chosen, local_tile[:, None] + 1, 0), axis=0) - 1
    has_left = place > 0
    has_right = place < count - 1
    asked = lax.all_to_all(
        request.reshape(count, capacity), "tok", split_axis=0, concat_axis=0, tiled=True
    ).reshape(slots)
    pair = jnp.stack([keys, values])
    pair_tiles = pair.reshape(2, tiles_here, KT, heads_here, head_dim)
    served = jnp.take(pair_tiles, jnp.clip(asked, 0, tiles_here - 1), axis=1)
    served = jnp.where((asked >= 0)[None, :, None, None, None], served, jnp.zeros((), jnp.bfloat16))
    fetched = lax.all_to_all(
        served.reshape(2, count, capacity, KT, heads_here, head_dim),
        "tok",
        split_axis=1,
        concat_axis=1,
        tiled=True,
    )
    fetched = fetched.reshape(2, slots, KT, heads_here, head_dim)
    far_pair = jnp.take(fetched, position, axis=1).reshape(2, ncrit * KT, heads_here, head_dim)
    window = padded(pair, (("tok", 1),), KT)
    key_pair = jnp.concatenate([window, far_pair], axis=1)
    valid = jnp.concatenate(
        [
            jnp.broadcast_to(has_left, (KT,)),
            jnp.ones((tok_rows,), bool),
            jnp.broadcast_to(has_right, (KT,)),
            jnp.repeat(used, KT),
        ]
    )
    scale = head_dim ** (-0.5)
    key_all = key_pair[0]
    value_all = key_pair[1]
    scores = (
        jnp.einsum("qhd,khd->hqk", queries, key_all, preferred_element_type=jnp.float32) * scale
    )
    scores = jnp.where(valid[None, None, :], scores, -1e30)
    top = jnp.max(scores, axis=-1, keepdims=True)
    probs = jnp.exp(scores - top)
    probs = probs / jnp.sum(probs, axis=-1, keepdims=True)
    probs_b = probs.astype(jnp.bfloat16)
    dprob = jnp.einsum("qhd,khd->hqk", d_attn, value_all, preferred_element_type=jnp.float32)
    delta = jnp.sum(probs * dprob, axis=-1, keepdims=True)
    dscore = (probs * (dprob - delta) * scale).astype(jnp.bfloat16)
    grad_q = jnp.einsum("hqk,khd->qhd", dscore, key_all, preferred_element_type=jnp.float32).astype(
        jnp.bfloat16
    )
    part_k = jnp.einsum("hqk,qhd->khd", dscore, queries, preferred_element_type=jnp.float32)
    part_v = jnp.einsum("hqk,qhd->khd", probs_b, d_attn, preferred_element_type=jnp.float32)
    grads = jnp.stack([part_k, part_v]) * valid.astype(jnp.float32)[None, :, None, None]
    left_part = grads[:, :KT]
    own_part = grads[:, KT : KT + tok_rows]
    right_part = grads[:, KT + tok_rows : 2 * KT + tok_rows]
    far_part = grads[:, 2 * KT + tok_rows :].reshape(2, ncrit, row_len)
    slotted = jnp.einsum(
        "cs,ecr->esr", chosen.astype(jnp.float32), far_part, precision=lax.Precision.HIGHEST
    )
    returned = lax.all_to_all(
        slotted.reshape(2, count, capacity, row_len).astype(jnp.bfloat16),
        "tok",
        split_axis=1,
        concat_axis=1,
        tiled=True,
    ).astype(jnp.float32)
    returned = returned.reshape(2, slots, row_len)
    owned = (asked[None, :] == jnp.arange(tiles_here)[:, None]).astype(jnp.float32)
    added = jnp.einsum("ts,esr->etr", owned, returned, precision=lax.Precision.HIGHEST)
    total = own_part + added.reshape(2, tok_rows, heads_here, head_dim)
    from_next = shifted(left_part.astype(jnp.bfloat16), "tok", -1).astype(left_part.dtype)
    from_prev = shifted(right_part.astype(jnp.bfloat16), "tok", 1).astype(right_part.dtype)
    total = total + jnp.pad(from_next, ((0, 0), (tok_rows - KT, 0), (0, 0), (0, 0)))
    total = total + jnp.pad(from_prev, ((0, 0), (0, tok_rows - KT), (0, 0), (0, 0)))
    return (grad_q, total[0].astype(jnp.bfloat16), total[1].astype(jnp.bfloat16))


def solution(mesh):
    return jax.shard_map(
        shards,
        mesh=mesh,
        in_specs=(
            P("tok", "head", None),
            P("tok", "head", None),
            P("tok", "head", None),
            P("tok", "head"),
            P("head", None),
            P("tok", None),
        ),
        out_specs=(P("tok", "head", None), P("tok", "head", None), P("tok", "head", None)),
        check_vma=False,
    )
```

```python
import functools

import jax
import jax.numpy as jnp
from jax import lax
from jax.experimental import pallas as pl
from jax.experimental.pallas import tpu as pltpu
from jax.sharding import PartitionSpec as P

KT = 16
LANES = 128
MASKED = -1e30
MESH = pl.DeviceIdType.MESH
NT = (((1,), (1,)), ((), ()))


def owner_of(h, group, count, heads):
    gap = count - heads
    odd = group % 2
    late = jnp.where(h >= heads // 2, gap, 0)
    return h + jnp.where(odd == 1, late, gap // 2)


def head_of(me, group, count, heads):
    gap = count - heads
    half = heads // 2
    odd = group % 2
    even_head = me - gap // 2
    odd_head = jnp.where(me < half, me, me - gap)
    even_owns = (even_head >= 0) & (even_head < heads)
    odd_owns = (me < half) | (me >= half + gap)
    owns = ((odd == 1) & odd_owns) | ((odd == 0) & even_owns)
    head = jnp.where(odd == 1, odd_head, even_head)
    return jnp.clip(head, 0, heads - 1), owns


def by_head_kernel(
    count, groups, ncrit, crit, q_in, k_in, v_in, go_in, w_in, grads,
    q_all, k_all, v_all, d_all, info_own, info_all, info, go_all, w_all, acc, d_own, onehot, k_sel,
    k_turned, v_sel, weights, scores, dprob, inverse, dk_part, dv_part, dq_st, dk_st, dv_st,
    info_sem, send_in, recv_in, send_go, recv_go, w_sem, send_out, recv_out,
):
    heads, rows, dim = q_in.shape
    tiles_here = rows // KT
    width = go_in.shape[1]
    me = lax.axis_index("tok")
    group = lax.axis_index("head")
    head, owns = head_of(me, group, count, heads)

    barrier = pltpu.get_barrier_semaphore()
    for step in range(1, count):
        pl.semaphore_signal(
            barrier, inc=1, device_id=((me + step) % count, group), device_id_type=MESH
        )
    mate = group + 1 - 2 * (group % 2)
    across = (group + groups // 2) % groups
    for other in (mate, across):
        pl.semaphore_signal(barrier, inc=1, device_id=(me, other), device_id_type=MESH)
    loads = []
    for s in range(groups):
        load = pltpu.make_async_copy(w_in.at[:, pl.ds(s * width, width)], w_all.at[s], w_sem.at[s])
        load.start()
        loads.append(load)
    near = tiles_here + 2
    slots = weights.shape[1] // KT
    chunks = weights.shape[1] // rows
    lane = lax.broadcasted_iota(jnp.int32, (8, LANES), 1)
    first = me * tiles_here - 1
    tile_in = first + lane
    tile_in = jnp.where((lane < near) & (tile_in >= 0) & (tile_in < count * tiles_here), tile_in, -1)
    slot_of = jnp.where((lane >= first) & (lane < first + near), lane - first, slots - 1)
    for c in range(ncrit):
        tile_in = jnp.where(lane == near + c, crit[0, c], tile_in)
        slot_of = jnp.where(lane == crit[0, c], near + c, slot_of)
    row = lax.broadcasted_iota(jnp.int32, (8, LANES), 0)
    info_own[...] = jnp.where(row == 0, jnp.maximum(tile_in, 0), jnp.where(row == 1, slot_of, tile_in))
    pl.semaphore_wait(barrier, count - 1 + 2)

    def go_copy(step):
        to = across if step == 2 else mate
        shard = across if step == 3 else group
        return pltpu.make_async_remote_copy(
            src_ref=go_all.at[across] if step == 3 else go_in,
            dst_ref=go_all.at[shard],
            send_sem=send_go.at[step],
            recv_sem=recv_go.at[step],
            device_id=(me, to),
            device_id_type=MESH,
        )

    go_copy(2).start()
    go_copy(1).start()
    own_go = pltpu.make_async_copy(go_in, go_all.at[group], recv_go.at[0])
    own_go.start()

    here = pl.ds(pl.multiple_of(me * rows, rows), rows)
    own_tiles = pl.ds(me * tiles_here, tiles_here)

    def target(i):
        half = heads // 2
        far = jnp.where(me < count // 2, half, 0)
        h = (far + (i % half + me) % half + (i // half) * half) % heads
        return h, owner_of(h, group, count, heads)

    def in_copy(kind, src, dst, h, owner):
        return pltpu.make_async_remote_copy(
            src_ref=src,
            dst_ref=dst,
            send_sem=send_in.at[kind, h],
            recv_sem=recv_in.at[kind, me],
            device_id=(owner, group),
            device_id_type=MESH,
        )

    def send(kind, src, dst, h, owner):
        @pl.when(owner != me)
        def _():
            in_copy(kind, src, dst, h, owner).start()

        @pl.when(owner == me)
        def _():
            pltpu.make_async_copy(src, dst, recv_in.at[kind, me]).start()

    for i in range(heads):
        h, owner = target(i)
        send(4, info_own, info_all.at[me], h, owner)
        send(0, k_in.at[h], k_all.at[own_tiles], h, owner)
    for i in range(heads):
        h, owner = target(i)
        send(1, q_in.at[h], q_all.at[here], h, owner)
    for i in range(heads):
        h, owner = target(i)
        send(2, v_in.at[h], v_all.at[own_tiles], h, owner)

    for step in range(groups):
        src = (group, mate, across, (mate + groups // 2) % groups)[step]
        if step == 0:
            own_go.wait()
        else:
            go_copy(step).wait_recv()
        if step == 2:
            go_copy(3).start()
        if step == 0:
            for load in loads:
                load.wait()
        part = lax.dot_general(
            go_all[src], w_all[src], NT, preferred_element_type=jnp.float32
        )
        if step == 0:
            acc[...] = part
        elif step < groups - 1:
            acc[...] += part
        else:
            done = (acc[...] + part).astype(jnp.bfloat16)
            for h in range(heads):
                d_own[h] = done[:, h * dim : (h + 1) * dim]
    for i in range(heads):
        h, owner = target(i)
        send(3, d_own.at[h], d_all.at[here], h, owner)

    def landed(kind, dst, b):
        in_copy_from = pltpu.make_async_remote_copy(
            src_ref=dst,
            dst_ref=dst,
            send_sem=send_in.at[kind, 0],
            recv_sem=recv_in.at[kind, b],
            device_id=((me + 1) % count, group),
            device_id_type=MESH,
        )
        in_copy_from.wait_recv()

    def block(b):
        return pl.ds(pl.multiple_of(b * rows, rows), rows)

    def tiles_of(b):
        return pl.ds(b * tiles_here, tiles_here)

    scale = dim ** (-0.5)
    low = me < count // 2

    def near_first(i):
        return jnp.where(low, i, count - 1 - i)

    @pl.when(owns)
    def _():
        def arrived(b, carry):
            landed(4, info_all.at[b], b)
            landed(0, k_all.at[tiles_of(b)], b)
            return carry

        lax.fori_loop(0, count, arrived, 0)
        to_scalars = pltpu.make_async_copy(info_all, info, info_sem)
        to_scalars.start()
        to_scalars.wait()

        def pick(source, chosen, b):
            for s in range(slots):
                chosen[b, s * KT : (s + 1) * KT, :] = source[info[b, 0, s]]

        def prepare(b, carry):
            pick(k_all, k_sel, b)
            for j in range(chunks):
                at = slice(j * rows, (j + 1) * rows)
                k_turned[b, j] = k_sel[b, at, :].T
            return carry

        lax.fori_loop(0, count, prepare, 0)
        for j in range(chunks):
            slot_id = lax.broadcasted_iota(jnp.int32, (rows, LANES), 1)
            of_row = j * (rows // KT) + lax.broadcasted_iota(jnp.int32, (rows, LANES), 0) // KT
            onehot[j * rows : (j + 1) * rows, :] = jnp.where(slot_id == of_row, 1.0, 0.0).astype(
                jnp.bfloat16
            )

        def forward(i, carry):
            b = near_first(i)
            landed(1, q_all.at[block(b)], b)
            bias = jnp.where(info_all[b][2:3, :] >= 0, 0.0, MASKED)
            bias = jnp.broadcast_to(bias, (rows, LANES)).astype(jnp.bfloat16)
            query = jnp.concatenate([q_all[block(b), :], bias], axis=1)
            top = jnp.full((8, rows), MASKED, jnp.float32)
            for j in range(chunks):
                at = slice(j * rows, (j + 1) * rows)
                key = jnp.concatenate([k_sel[b, at, :], onehot[at, :]], axis=1)
                s = lax.dot_general(key, query, NT, preferred_element_type=jnp.float32)
                scores[at, :] = s
                top = jnp.maximum(top, jnp.max(s.reshape(rows // 8, 8, rows), axis=0))
            top = jnp.max(top, axis=0, keepdims=True)
            factor = scale * 1.4426950408889634
            summed = jnp.zeros((8, rows), jnp.float32)
            for j in range(chunks):
                at = slice(j * rows, (j + 1) * rows)
                e = jnp.exp2((scores[at, :] - top) * factor)
                weights[b, at, :] = e.astype(jnp.bfloat16)
                summed = summed + jnp.sum(e.reshape(rows // 8, 8, rows), axis=0)
            inv = 1.0 / jnp.sum(summed, axis=0, keepdims=True)
            inverse[b] = jnp.broadcast_to(inv, (8, rows))
            return carry

        lax.fori_loop(0, count, forward, 0)

        def values_in(b, carry):
            landed(2, v_all.at[tiles_of(b)], b)
            return carry

        lax.fori_loop(0, count, values_in, 0)

        def pick_values(b, carry):
            pick(v_all, v_sel, b)
            return carry

        lax.fori_loop(0, count, pick_values, 0)

        def backward(i, carry):
            b = near_first(i)
            landed(3, d_all.at[block(b)], b)
            d_b = d_all[block(b), :]
            q_b = q_all[block(b), :]
            inv = inverse[b][0:1, :]
            delta = jnp.zeros((8, rows), jnp.float32)
            for j in range(chunks):
                at = slice(j * rows, (j + 1) * rows)
                dp = lax.dot_general(v_sel[b, at, :], d_b, NT, preferred_element_type=jnp.float32)
                dprob[at, :] = dp
                w = weights[b, at, :].astype(jnp.float32) * dp
                delta = delta + jnp.sum(w.reshape(rows // 8, 8, rows), axis=0)
            delta = jnp.sum(delta, axis=0, keepdims=True) * inv
            dq = jnp.zeros((dim, rows), jnp.float32)
            for j in range(chunks):
                at = slice(j * rows, (j + 1) * rows)
                p = weights[b, at, :].astype(jnp.float32) * inv
                ds = (p * (dprob[at, :] - delta)).astype(jnp.bfloat16)
                dv = jnp.dot(p.astype(jnp.bfloat16), d_b, preferred_element_type=jnp.float32)
                dk = jnp.dot(ds, q_b, preferred_element_type=jnp.float32)
                part = slice(j * tiles_here, (j + 1) * tiles_here)
                dv_part[b, part] = dv.reshape(tiles_here, KT, dim)
                dk_part[b, part] = dk.reshape(tiles_here, KT, dim)
                dq = dq + jnp.dot(k_turned[b, j], ds, preferred_element_type=jnp.float32)
            dq_st[block(b), :] = (dq * scale).T.astype(jnp.bfloat16)
            give(0, dq_st, b)
            return carry

        def out_copy(kind, staged, b):
            return pltpu.make_async_remote_copy(
                src_ref=staged.at[block(b)],
                dst_ref=grads.at[kind, head],
                send_sem=send_out.at[kind, b],
                recv_sem=recv_out.at[kind, head],
                device_id=(b, group),
                device_id_type=MESH,
            )

        def give(kind, staged, b):
            @pl.when(b != me)
            def _():
                out_copy(kind, staged, b).start()

            @pl.when(b == me)
            def _():
                pltpu.make_async_copy(
                    staged.at[block(b)], grads.at[kind, head], recv_out.at[kind, head]
                ).start()

        lax.fori_loop(0, count, backward, 0)

        def finish(i, carry):
            b = near_first(count - 1 - i)
            for t in range(tiles_here):
                dk = jnp.zeros((KT, dim), jnp.float32)
                dv = jnp.zeros((KT, dim), jnp.float32)
                for c in range(count):
                    slot = info[c, 1, b * tiles_here + t]
                    dk = dk + dk_part[c, slot]
                    dv = dv + dv_part[c, slot]
                at = pl.ds(pl.multiple_of(b * rows + t * KT, KT), KT)
                dk_st[at, :] = (dk * scale).astype(jnp.bfloat16)
                dv_st[at, :] = dv.astype(jnp.bfloat16)
            give(1, dk_st, b)
            give(2, dv_st, b)
            return carry

        lax.fori_loop(0, count, finish, 0)

        def sent(b, carry):
            @pl.when(b != me)
            def _():
                for kind, staged in ((0, dq_st), (1, dk_st), (2, dv_st)):
                    out_copy(kind, staged, b).wait_send()

            return carry

        lax.fori_loop(0, count, sent, 0)

    for step in range(1, groups):
        go_copy(step).wait_send()
    for h in range(heads):
        owner = owner_of(h, group, count, heads)

        @pl.when(owner != me)
        def _():
            in_copy(0, k_in.at[h], k_all.at[own_tiles], h, owner).wait_send()
            in_copy(1, q_in.at[h], q_all.at[here], h, owner).wait_send()
            in_copy(2, v_in.at[h], v_all.at[own_tiles], h, owner).wait_send()
            in_copy(3, d_own.at[h], d_all.at[here], h, owner).wait_send()
            in_copy(4, info_own, info_all.at[me], h, owner).wait_send()

        for kind in range(3):
            pltpu.make_async_remote_copy(
                src_ref=grads.at[kind, h],
                dst_ref=grads.at[kind, h],
                send_sem=send_out.at[kind, 0],
                recv_sem=recv_out.at[kind, h],
                device_id=((me + 1) % count, group),
                device_id_type=MESH,
            ).wait_recv()


def by_head(queries, keys, values, grad_out, w_out, crit):
    rows, heads, dim = queries.shape
    count = lax.axis_size("tok")
    groups = lax.axis_size("head")
    total = count * rows
    width = grad_out.shape[1]
    tiles_here = rows // KT
    chosen = ((tiles_here + 2 + crit.shape[1]) // tiles_here + 1) * rows
    bf16, f32 = jnp.bfloat16, jnp.float32
    hbm = pl.BlockSpec(memory_space=pl.ANY)
    vmem, dma = pltpu.VMEM, pltpu.SemaphoreType.DMA
    out = jax.ShapeDtypeStruct((3, heads, rows, dim), bf16)
    grads = pl.pallas_call(
        functools.partial(by_head_kernel, count, groups, crit.shape[1]),
        out_shape=out,
        in_specs=[pl.BlockSpec(memory_space=pltpu.SMEM)] + [hbm] * 5,
        out_specs=hbm,
        scratch_shapes=[
            vmem((total, dim), bf16),
            vmem((total // KT, KT, dim), bf16),
            vmem((total // KT, KT, dim), bf16),
            vmem((total, dim), bf16),
            vmem((8, LANES), jnp.int32),
            vmem((count, 8, LANES), jnp.int32),
            pltpu.SMEM((count, 8, LANES), jnp.int32),
            vmem((groups, rows, width), bf16),
            vmem((groups, w_out.shape[0], width), bf16),
            vmem((rows, heads * dim), f32),
            vmem((heads, rows, dim), bf16),
            vmem((chosen, LANES), bf16),
            vmem((count, chosen, dim), bf16),
            vmem((count, chosen // rows, dim, rows), bf16),
            vmem((count, chosen, dim), bf16),
            vmem((count, chosen, rows), bf16),
            vmem((chosen, rows), f32),
            vmem((chosen, rows), f32),
            vmem((count, 8, rows), f32),
            vmem((count, chosen // KT, KT, dim), f32),
            vmem((count, chosen // KT, KT, dim), f32),
            vmem((total, dim), bf16),
            vmem((total, dim), bf16),
            vmem((total, dim), bf16),
            dma,
            dma((5, heads)),
            dma((5, count)),
            dma((groups,)),
            dma((groups,)),
            dma((groups,)),
            dma((3, count)),
            dma((3, heads)),
        ],
        compiler_params=pltpu.CompilerParams(
            collective_id=0, has_side_effects=True, vmem_limit_bytes=63 * 2**20 + 2**19
        ),
    )(
        crit,
        jnp.transpose(queries, (1, 0, 2)),
        jnp.transpose(keys, (1, 0, 2)).reshape(heads, tiles_here, KT, dim),
        jnp.transpose(values, (1, 0, 2)).reshape(heads, tiles_here, KT, dim),
        grad_out,
        w_out,
    )
    return tuple(jnp.transpose(grads[kind], (1, 0, 2)) for kind in range(3))


def padded(cells, sides, width):
    for axis, dim in sides:
        count = lax.axis_size(axis)
        ends = count - 1
        head = lax.slice_in_dim(cells, 0, width, axis=dim)
        tail = lax.slice_in_dim(cells, cells.shape[dim] - width, cells.shape[dim], axis=dim)
        cells = jnp.concatenate(
            [
                lax.ppermute(tail, axis, [(i, (i + 1) % count) for i in range(ends)]),
                cells,
                lax.ppermute(head, axis, [((i + 1) % count, i) for i in range(ends)]),
            ],
            axis=dim,
        )
    return cells


def shifted(value, axis, steps):
    count = lax.axis_size(axis)
    leading, last = (max(0, -steps), min(count, count - steps))
    return lax.ppermute(value, axis, [(source, source + steps) for source in range(leading, last)])


def shards(queries, keys, values, grad_out, w_out, crit):
    tok_rows, heads_here, head_dim = queries.shape
    width_here = heads_here * head_dim
    count = lax.axis_size("tok")
    place = lax.axis_index("tok")
    tiles_here = tok_rows // KT
    if lax.axis_size("head") == 4 and heads_here <= count <= 2 * heads_here and count * tiles_here <= LANES and tok_rows % KT == 0 and tiles_here + crit.shape[1] < 110:
        return by_head(queries, keys, values, grad_out, w_out, crit)
    ncrit = crit.shape[1]
    capacity = (ncrit + count - 4) // (count - 3)
    slots = count * capacity
    row_len = KT * width_here
    d_attn = lax.dot_general(
        lax.all_gather(grad_out, "head", axis=1, tiled=True),
        w_out,
        (((1,), (1,)), ((), ())),
        preferred_element_type=jnp.float32,
    )
    d_attn = d_attn.astype(jnp.bfloat16).reshape(tok_rows, heads_here, head_dim)
    tiles = crit[0]
    used = tiles >= 0
    owner = jnp.where(used, tiles // tiles_here, -1)
    local_tile = jnp.where(used, tiles % tiles_here, 0)
    order = jnp.arange(ncrit)
    earlier = (owner[:, None] == owner[None, :]) & (order[:, None] > order[None, :]) & used[None, :]
    slot = jnp.sum(earlier.astype(jnp.int32), axis=1)
    position = jnp.where(used, owner * capacity + slot, 0)
    slot_ids = jnp.arange(slots)
    chosen = used[:, None] & (position[:, None] == slot_ids[None, :])
    request = jnp.sum(jnp.where(chosen, local_tile[:, None] + 1, 0), axis=0) - 1
    has_left = place > 0
    has_right = place < count - 1
    asked = lax.all_to_all(
        request.reshape(count, capacity), "tok", split_axis=0, concat_axis=0, tiled=True
    ).reshape(slots)
    pair = jnp.stack([keys, values])
    pair_tiles = pair.reshape(2, tiles_here, KT, heads_here, head_dim)
    served = jnp.take(pair_tiles, jnp.clip(asked, 0, tiles_here - 1), axis=1)
    served = jnp.where((asked >= 0)[None, :, None, None, None], served, jnp.zeros((), jnp.bfloat16))
    fetched = lax.all_to_all(
        served.reshape(2, count, capacity, KT, heads_here, head_dim),
        "tok",
        split_axis=1,
        concat_axis=1,
        tiled=True,
    )
    fetched = fetched.reshape(2, slots, KT, heads_here, head_dim)
    far_pair = jnp.take(fetched, position, axis=1).reshape(2, ncrit * KT, heads_here, head_dim)
    window = padded(pair, (("tok", 1),), KT)
    key_pair = jnp.concatenate([window, far_pair], axis=1)
    valid = jnp.concatenate(
        [
            jnp.broadcast_to(has_left, (KT,)),
            jnp.ones((tok_rows,), bool),
            jnp.broadcast_to(has_right, (KT,)),
            jnp.repeat(used, KT),
        ]
    )
    scale = head_dim ** (-0.5)
    key_all = key_pair[0]
    value_all = key_pair[1]
    scores = (
        jnp.einsum("qhd,khd->hqk", queries, key_all, preferred_element_type=jnp.float32) * scale
    )
    scores = jnp.where(valid[None, None, :], scores, -1e30)
    top = jnp.max(scores, axis=-1, keepdims=True)
    probs = jnp.exp(scores - top)
    probs = probs / jnp.sum(probs, axis=-1, keepdims=True)
    probs_b = probs.astype(jnp.bfloat16)
    dprob = jnp.einsum("qhd,khd->hqk", d_attn, value_all, preferred_element_type=jnp.float32)
    delta = jnp.sum(probs * dprob, axis=-1, keepdims=True)
    dscore = (probs * (dprob - delta) * scale).astype(jnp.bfloat16)
    grad_q = jnp.einsum("hqk,khd->qhd", dscore, key_all, preferred_element_type=jnp.float32).astype(
        jnp.bfloat16
    )
    part_k = jnp.einsum("hqk,qhd->khd", dscore, queries, preferred_element_type=jnp.float32)
    part_v = jnp.einsum("hqk,qhd->khd", probs_b, d_attn, preferred_element_type=jnp.float32)
    grads = jnp.stack([part_k, part_v]) * valid.astype(jnp.float32)[None, :, None, None]
    left_part = grads[:, :KT]
    own_part = grads[:, KT : KT + tok_rows]
    right_part = grads[:, KT + tok_rows : 2 * KT + tok_rows]
    far_part = grads[:, 2 * KT + tok_rows :].reshape(2, ncrit, row_len)
    slotted = jnp.einsum(
        "cs,ecr->esr", chosen.astype(jnp.float32), far_part, precision=lax.Precision.HIGHEST
    )
    returned = lax.all_to_all(
        slotted.reshape(2, count, capacity, row_len).astype(jnp.bfloat16),
        "tok",
        split_axis=1,
        concat_axis=1,
        tiled=True,
    ).astype(jnp.float32)
    returned = returned.reshape(2, slots, row_len)
    owned = (asked[None, :] == jnp.arange(tiles_here)[:, None]).astype(jnp.float32)
    added = jnp.einsum("ts,esr->etr", owned, returned, precision=lax.Precision.HIGHEST)
    total = own_part + added.reshape(2, tok_rows, heads_here, head_dim)
    from_next = shifted(left_part.astype(jnp.bfloat16), "tok", -1).astype(left_part.dtype)
    from_prev = shifted(right_part.astype(jnp.bfloat16), "tok", 1).astype(right_part.dtype)
    total = total + jnp.pad(from_next, ((0, 0), (tok_rows - KT, 0), (0, 0), (0, 0)))
    total = total + jnp.pad(from_prev, ((0, 0), (0, tok_rows - KT), (0, 0), (0, 0)))
    return (grad_q, total[0].astype(jnp.bfloat16), total[1].astype(jnp.bfloat16))


def solution(mesh):
    return jax.shard_map(
        shards,
        mesh=mesh,
        in_specs=(
            P("tok", "head", None),
            P("tok", "head", None),
            P("tok", "head", None),
            P("tok", "head"),
            P("head", None),
            P("tok", None),
        ),
        out_specs=(P("tok", "head", None), P("tok", "head", None), P("tok", "head", None)),
        check_vma=False,
    )
```

```python
import functools

import jax
import jax.numpy as jnp
from jax import lax
from jax.experimental import pallas as pl
from jax.experimental.pallas import tpu as pltpu
from jax.sharding import PartitionSpec as P

KT = 16
LANES = 128
MASKED = -1e30
MESH = pl.DeviceIdType.MESH
NT = (((1,), (1,)), ((), ()))


def owner_of(h, group, count, heads):
    gap = count - heads
    odd = group % 2
    late = jnp.where(h >= heads // 2, gap, 0)
    return h + jnp.where(odd == 1, late, gap // 2)


def head_of(me, group, count, heads):
    gap = count - heads
    half = heads // 2
    odd = group % 2
    even_head = me - gap // 2
    odd_head = jnp.where(me < half, me, me - gap)
    even_owns = (even_head >= 0) & (even_head < heads)
    odd_owns = (me < half) | (me >= half + gap)
    owns = ((odd == 1) & odd_owns) | ((odd == 0) & even_owns)
    head = jnp.where(odd == 1, odd_head, even_head)
    return jnp.clip(head, 0, heads - 1), owns


def by_head_kernel(
    count, groups, ncrit, crit, q_in, k_in, v_in, go_in, w_in, grads,
    q_all, k_all, v_all, d_all, info_own, info_all, info, go_all, w_all, acc, d_own, onehot, k_sel,
    k_turned, v_sel, weights, scores, dprob, inverse, dk_part, dv_part, dq_st, dk_st, dv_st,
    info_sem, send_in, recv_in, send_go, recv_go, w_sem, send_out, recv_out,
):
    heads, rows, dim = q_in.shape
    tiles_here = rows // KT
    width = go_in.shape[1]
    me = lax.axis_index("tok")
    group = lax.axis_index("head")
    head, owns = head_of(me, group, count, heads)

    barrier = pltpu.get_barrier_semaphore()
    for step in range(1, count):
        pl.semaphore_signal(
            barrier, inc=1, device_id=((me + step) % count, group), device_id_type=MESH
        )
    mate = group + 1 - 2 * (group % 2)
    across = (group + groups // 2) % groups
    for other in (mate, across):
        pl.semaphore_signal(barrier, inc=1, device_id=(me, other), device_id_type=MESH)
    loads = []
    for s in range(groups):
        load = pltpu.make_async_copy(w_in.at[:, pl.ds(s * width, width)], w_all.at[s], w_sem.at[s])
        load.start()
        loads.append(load)
    near = tiles_here + 2
    slots = weights.shape[1] // KT
    chunks = weights.shape[1] // rows
    lane = lax.broadcasted_iota(jnp.int32, (8, LANES), 1)
    first = me * tiles_here - 1
    tile_in = first + lane
    tile_in = jnp.where((lane < near) & (tile_in >= 0) & (tile_in < count * tiles_here), tile_in, -1)
    slot_of = jnp.where((lane >= first) & (lane < first + near), lane - first, slots - 1)
    for c in range(ncrit):
        tile_in = jnp.where(lane == near + c, crit[0, c], tile_in)
        slot_of = jnp.where(lane == crit[0, c], near + c, slot_of)
    row = lax.broadcasted_iota(jnp.int32, (8, LANES), 0)
    info_own[...] = jnp.where(row == 0, jnp.maximum(tile_in, 0), jnp.where(row == 1, slot_of, tile_in))
    pl.semaphore_wait(barrier, count - 1 + 2)

    def go_copy(step):
        to = across if step == 2 else mate
        shard = across if step == 3 else group
        return pltpu.make_async_remote_copy(
            src_ref=go_all.at[across] if step == 3 else go_in,
            dst_ref=go_all.at[shard],
            send_sem=send_go.at[step],
            recv_sem=recv_go.at[step],
            device_id=(me, to),
            device_id_type=MESH,
        )

    go_copy(2).start()
    go_copy(1).start()
    own_go = pltpu.make_async_copy(go_in, go_all.at[group], recv_go.at[0])
    own_go.start()

    here = pl.ds(pl.multiple_of(me * rows, rows), rows)
    own_tiles = pl.ds(me * tiles_here, tiles_here)

    def target(i):
        half = heads // 2
        far = jnp.where(me < count // 2, half, 0)
        h = (far + (i % half + me) % half + (i // half) * half) % heads
        return h, owner_of(h, group, count, heads)

    def in_copy(kind, src, dst, h, owner):
        return pltpu.make_async_remote_copy(
            src_ref=src,
            dst_ref=dst,
            send_sem=send_in.at[kind, h],
            recv_sem=recv_in.at[kind, me],
            device_id=(owner, group),
            device_id_type=MESH,
        )

    def send(kind, src, dst, h, owner):
        @pl.when(owner != me)
        def _():
            in_copy(kind, src, dst, h, owner).start()

        @pl.when(owner == me)
        def _():
            pltpu.make_async_copy(src, dst, recv_in.at[kind, me]).start()

    for i in range(heads):
        h, owner = target(i)
        send(4, info_own, info_all.at[me], h, owner)
        send(0, k_in.at[h], k_all.at[own_tiles], h, owner)
    for i in range(heads):
        h, owner = target(i)
        send(1, q_in.at[h], q_all.at[here], h, owner)
    for i in range(heads):
        h, owner = target(i)
        send(2, v_in.at[h], v_all.at[own_tiles], h, owner)

    for step in range(groups):
        src = (group, mate, across, (mate + groups // 2) % groups)[step]
        if step == 0:
            own_go.wait()
        else:
            go_copy(step).wait_recv()
        if step == 2:
            go_copy(3).start()
        if step == 0:
            for load in loads:
                load.wait()
        part = lax.dot_general(
            go_all[src], w_all[src], NT, preferred_element_type=jnp.float32
        )
        if step == 0:
            acc[...] = part
        elif step < groups - 1:
            acc[...] += part
        else:
            done = (acc[...] + part).astype(jnp.bfloat16)
            for h in range(heads):
                d_own[h] = done[:, h * dim : (h + 1) * dim]
    for i in range(heads):
        h, owner = target(i)
        send(3, d_own.at[h], d_all.at[here], h, owner)

    def landed(kind, dst, b):
        in_copy_from = pltpu.make_async_remote_copy(
            src_ref=dst,
            dst_ref=dst,
            send_sem=send_in.at[kind, 0],
            recv_sem=recv_in.at[kind, b],
            device_id=((me + 1) % count, group),
            device_id_type=MESH,
        )
        in_copy_from.wait_recv()

    def block(b):
        return pl.ds(pl.multiple_of(b * rows, rows), rows)

    def tiles_of(b):
        return pl.ds(b * tiles_here, tiles_here)

    scale = dim ** (-0.5)
    low = me < count // 2

    def near_first(i):
        return jnp.where(low, i, count - 1 - i)

    @pl.when(owns)
    def _():
        def arrived(b, carry):
            landed(4, info_all.at[b], b)
            landed(0, k_all.at[tiles_of(b)], b)
            return carry

        lax.fori_loop(0, count, arrived, 0)
        to_scalars = pltpu.make_async_copy(info_all, info, info_sem)
        to_scalars.start()
        to_scalars.wait()

        def pick(source, chosen, b):
            for s in range(slots):
                chosen[b, s * KT : (s + 1) * KT, :] = source[info[b, 0, s]]

        def prepare(b, carry):
            pick(k_all, k_sel, b)
            for j in range(chunks):
                at = slice(j * rows, (j + 1) * rows)
                k_turned[b, j] = k_sel[b, at, :].T
            return carry

        lax.fori_loop(0, count, prepare, 0)
        for j in range(chunks):
            slot_id = lax.broadcasted_iota(jnp.int32, (rows, LANES), 1)
            of_row = j * (rows // KT) + lax.broadcasted_iota(jnp.int32, (rows, LANES), 0) // KT
            onehot[j * rows : (j + 1) * rows, :] = jnp.where(slot_id == of_row, 1.0, 0.0).astype(
                jnp.bfloat16
            )

        def forward(i, carry):
            b = near_first(i)
            landed(1, q_all.at[block(b)], b)
            bias = jnp.where(info_all[b][2:3, :] >= 0, 0.0, MASKED)
            bias = jnp.broadcast_to(bias, (rows, LANES)).astype(jnp.bfloat16)
            query = jnp.concatenate([q_all[block(b), :], bias], axis=1)
            top = jnp.full((8, rows), MASKED, jnp.float32)
            for j in range(chunks):
                at = slice(j * rows, (j + 1) * rows)
                key = jnp.concatenate([k_sel[b, at, :], onehot[at, :]], axis=1)
                s = lax.dot_general(key, query, NT, preferred_element_type=jnp.float32)
                scores[at, :] = s
                top = jnp.maximum(top, jnp.max(s.reshape(rows // 8, 8, rows), axis=0))
            top = jnp.max(top, axis=0, keepdims=True)
            factor = scale * 1.4426950408889634
            summed = jnp.zeros((8, rows), jnp.float32)
            for j in range(chunks):
                at = slice(j * rows, (j + 1) * rows)
                e = jnp.exp2((scores[at, :] - top) * factor)
                weights[b, at, :] = e.astype(jnp.bfloat16)
                summed = summed + jnp.sum(e.reshape(rows // 8, 8, rows), axis=0)
            inv = 1.0 / jnp.sum(summed, axis=0, keepdims=True)
            inverse[b] = jnp.broadcast_to(inv, (8, rows))
            return carry

        lax.fori_loop(0, count, forward, 0)

        def values_in(b, carry):
            landed(2, v_all.at[tiles_of(b)], b)
            return carry

        lax.fori_loop(0, count, values_in, 0)

        def pick_values(b, carry):
            pick(v_all, v_sel, b)
            return carry

        lax.fori_loop(0, count, pick_values, 0)

        def backward(i, carry):
            b = near_first(i)
            landed(3, d_all.at[block(b)], b)
            d_b = d_all[block(b), :]
            q_b = q_all[block(b), :]
            inv = inverse[b][0:1, :]
            delta = jnp.zeros((8, rows), jnp.float32)
            for j in range(chunks):
                at = slice(j * rows, (j + 1) * rows)
                dp = lax.dot_general(v_sel[b, at, :], d_b, NT, preferred_element_type=jnp.float32)
                dprob[at, :] = dp
                w = weights[b, at, :].astype(jnp.float32) * dp
                delta = delta + jnp.sum(w.reshape(rows // 8, 8, rows), axis=0)
            delta = jnp.sum(delta, axis=0, keepdims=True) * inv
            dq = jnp.zeros((dim, rows), jnp.float32)
            for j in range(chunks):
                at = slice(j * rows, (j + 1) * rows)
                p = weights[b, at, :].astype(jnp.float32) * inv
                ds = (p * (dprob[at, :] - delta)).astype(jnp.bfloat16)
                dv = jnp.dot(p.astype(jnp.bfloat16), d_b, preferred_element_type=jnp.float32)
                dk = jnp.dot(ds, q_b, preferred_element_type=jnp.float32)
                part = slice(j * tiles_here, (j + 1) * tiles_here)
                dv_part[b, part] = dv.reshape(tiles_here, KT, dim)
                dk_part[b, part] = dk.reshape(tiles_here, KT, dim)
                dq = dq + jnp.dot(k_turned[b, j], ds, preferred_element_type=jnp.float32)
            dq_st[block(b), :] = (dq * scale).T.astype(jnp.bfloat16)
            give(0, dq_st, b)
            return carry

        def out_copy(kind, staged, b):
            return pltpu.make_async_remote_copy(
                src_ref=staged.at[block(b)],
                dst_ref=grads.at[kind, head],
                send_sem=send_out.at[kind, b],
                recv_sem=recv_out.at[kind, head],
                device_id=(b, group),
                device_id_type=MESH,
            )

        def give(kind, staged, b):
            @pl.when(b != me)
            def _():
                out_copy(kind, staged, b).start()

            @pl.when(b == me)
            def _():
                pltpu.make_async_copy(
                    staged.at[block(b)], grads.at[kind, head], recv_out.at[kind, head]
                ).start()

        lax.fori_loop(0, count, backward, 0)

        def finish(i, carry):
            b = near_first(count - 1 - i)
            for t in range(tiles_here):
                dk = jnp.zeros((KT, dim), jnp.float32)
                dv = jnp.zeros((KT, dim), jnp.float32)
                for c in range(count):
                    slot = info[c, 1, b * tiles_here + t]
                    dk = dk + dk_part[c, slot]
                    dv = dv + dv_part[c, slot]
                at = pl.ds(pl.multiple_of(b * rows + t * KT, KT), KT)
                dk_st[at, :] = (dk * scale).astype(jnp.bfloat16)
                dv_st[at, :] = dv.astype(jnp.bfloat16)
            give(1, dk_st, b)
            give(2, dv_st, b)
            return carry

        lax.fori_loop(0, count, finish, 0)

        def sent(b, carry):
            @pl.when(b != me)
            def _():
                for kind, staged in ((0, dq_st), (1, dk_st), (2, dv_st)):
                    out_copy(kind, staged, b).wait_send()

            return carry

        lax.fori_loop(0, count, sent, 0)

    for step in range(1, groups):
        go_copy(step).wait_send()
    for h in range(heads):
        owner = owner_of(h, group, count, heads)

        @pl.when(owner != me)
        def _():
            in_copy(0, k_in.at[h], k_all.at[own_tiles], h, owner).wait_send()
            in_copy(1, q_in.at[h], q_all.at[here], h, owner).wait_send()
            in_copy(2, v_in.at[h], v_all.at[own_tiles], h, owner).wait_send()
            in_copy(3, d_own.at[h], d_all.at[here], h, owner).wait_send()
            in_copy(4, info_own, info_all.at[me], h, owner).wait_send()

        for kind in range(3):
            pltpu.make_async_remote_copy(
                src_ref=grads.at[kind, h],
                dst_ref=grads.at[kind, h],
                send_sem=send_out.at[kind, 0],
                recv_sem=recv_out.at[kind, h],
                device_id=((me + 1) % count, group),
                device_id_type=MESH,
            ).wait_recv()


def split_kernel(grads, dq_out, dk_out, dv_out, held, sems):
    heads = grads.shape[1]
    pieces = [(kind, h) for kind in range(3) for h in range(heads)]
    outs = (dq_out, dk_out, dv_out)
    fetches = [
        pltpu.make_async_copy(grads.at[kind, h], held.at[kind, h], sems.at[0, kind, h])
        for kind, h in pieces
    ]
    stores = [
        pltpu.make_async_copy(held.at[kind, h], outs[kind].at[h], sems.at[1, kind, h])
        for kind, h in pieces
    ]
    for fetch in fetches:
        fetch.start()
    for fetch, store in zip(fetches, stores):
        fetch.wait()
        store.start()
    for store in stores:
        store.wait()


def by_head(queries, keys, values, grad_out, w_out, crit):
    rows, heads, dim = queries.shape
    count = lax.axis_size("tok")
    groups = lax.axis_size("head")
    total = count * rows
    width = grad_out.shape[1]
    tiles_here = rows // KT
    chosen = ((tiles_here + 2 + crit.shape[1]) // tiles_here + 1) * rows
    bf16, f32 = jnp.bfloat16, jnp.float32
    anywhere = pl.BlockSpec(memory_space=pl.ANY)
    vmem, dma = pltpu.VMEM, pltpu.SemaphoreType.DMA
    out = jax.ShapeDtypeStruct((3, heads, rows, dim), bf16)
    grads = pl.pallas_call(
        functools.partial(by_head_kernel, count, groups, crit.shape[1]),
        out_shape=out,
        in_specs=[pl.BlockSpec(memory_space=pltpu.SMEM)] + [anywhere] * 5,
        out_specs=anywhere,
        scratch_shapes=[
            vmem((total, dim), bf16),
            vmem((total // KT, KT, dim), bf16),
            vmem((total // KT, KT, dim), bf16),
            vmem((total, dim), bf16),
            vmem((8, LANES), jnp.int32),
            vmem((count, 8, LANES), jnp.int32),
            pltpu.SMEM((count, 8, LANES), jnp.int32),
            vmem((groups, rows, width), bf16),
            vmem((groups, w_out.shape[0], width), bf16),
            vmem((rows, heads * dim), f32),
            vmem((heads, rows, dim), bf16),
            vmem((chosen, LANES), bf16),
            vmem((count, chosen, dim), bf16),
            vmem((count, chosen // rows, dim, rows), bf16),
            vmem((count, chosen, dim), bf16),
            vmem((count, chosen, rows), bf16),
            vmem((chosen, rows), f32),
            vmem((chosen, rows), f32),
            vmem((count, 8, rows), f32),
            vmem((count, chosen // KT, KT, dim), f32),
            vmem((count, chosen // KT, KT, dim), f32),
            vmem((total, dim), bf16),
            vmem((total, dim), bf16),
            vmem((total, dim), bf16),
            dma,
            dma((5, heads)),
            dma((5, count)),
            dma((groups,)),
            dma((groups,)),
            dma((groups,)),
            dma((3, count)),
            dma((3, heads)),
        ],
        compiler_params=pltpu.CompilerParams(
            collective_id=0, has_side_effects=True, vmem_limit_bytes=63 * 2**20 + 2**19
        ),
    )(
        crit,
        jnp.transpose(queries, (1, 0, 2)),
        jnp.transpose(keys, (1, 0, 2)).reshape(heads, tiles_here, KT, dim),
        jnp.transpose(values, (1, 0, 2)).reshape(heads, tiles_here, KT, dim),
        grad_out,
        w_out,
    )
    one = jax.ShapeDtypeStruct((heads, rows, dim), bf16)
    grads = pl.pallas_call(
        split_kernel,
        out_shape=(one, one, one),
        in_specs=[anywhere],
        out_specs=(anywhere, anywhere, anywhere),
        scratch_shapes=[vmem((3, heads, rows, dim), bf16), dma((2, 3, heads))],
        compiler_params=pltpu.CompilerParams(vmem_limit_bytes=63 * 2**20 + 2**19),
    )(grads)
    return tuple(jnp.transpose(grad, (1, 0, 2)) for grad in grads)


def padded(cells, sides, width):
    for axis, dim in sides:
        count = lax.axis_size(axis)
        ends = count - 1
        head = lax.slice_in_dim(cells, 0, width, axis=dim)
        tail = lax.slice_in_dim(cells, cells.shape[dim] - width, cells.shape[dim], axis=dim)
        cells = jnp.concatenate(
            [
                lax.ppermute(tail, axis, [(i, (i + 1) % count) for i in range(ends)]),
                cells,
                lax.ppermute(head, axis, [((i + 1) % count, i) for i in range(ends)]),
            ],
            axis=dim,
        )
    return cells


def shifted(value, axis, steps):
    count = lax.axis_size(axis)
    leading, last = (max(0, -steps), min(count, count - steps))
    return lax.ppermute(value, axis, [(source, source + steps) for source in range(leading, last)])


def shards(queries, keys, values, grad_out, w_out, crit):
    tok_rows, heads_here, head_dim = queries.shape
    width_here = heads_here * head_dim
    count = lax.axis_size("tok")
    place = lax.axis_index("tok")
    tiles_here = tok_rows // KT
    if lax.axis_size("head") == 4 and heads_here <= count <= 2 * heads_here and count * tiles_here <= LANES and tok_rows % KT == 0 and tiles_here + crit.shape[1] < 110:
        return by_head(queries, keys, values, grad_out, w_out, crit)
    ncrit = crit.shape[1]
    capacity = (ncrit + count - 4) // (count - 3)
    slots = count * capacity
    row_len = KT * width_here
    d_attn = lax.dot_general(
        lax.all_gather(grad_out, "head", axis=1, tiled=True),
        w_out,
        (((1,), (1,)), ((), ())),
        preferred_element_type=jnp.float32,
    )
    d_attn = d_attn.astype(jnp.bfloat16).reshape(tok_rows, heads_here, head_dim)
    tiles = crit[0]
    used = tiles >= 0
    owner = jnp.where(used, tiles // tiles_here, -1)
    local_tile = jnp.where(used, tiles % tiles_here, 0)
    order = jnp.arange(ncrit)
    earlier = (owner[:, None] == owner[None, :]) & (order[:, None] > order[None, :]) & used[None, :]
    slot = jnp.sum(earlier.astype(jnp.int32), axis=1)
    position = jnp.where(used, owner * capacity + slot, 0)
    slot_ids = jnp.arange(slots)
    chosen = used[:, None] & (position[:, None] == slot_ids[None, :])
    request = jnp.sum(jnp.where(chosen, local_tile[:, None] + 1, 0), axis=0) - 1
    has_left = place > 0
    has_right = place < count - 1
    asked = lax.all_to_all(
        request.reshape(count, capacity), "tok", split_axis=0, concat_axis=0, tiled=True
    ).reshape(slots)
    pair = jnp.stack([keys, values])
    pair_tiles = pair.reshape(2, tiles_here, KT, heads_here, head_dim)
    served = jnp.take(pair_tiles, jnp.clip(asked, 0, tiles_here - 1), axis=1)
    served = jnp.where((asked >= 0)[None, :, None, None, None], served, jnp.zeros((), jnp.bfloat16))
    fetched = lax.all_to_all(
        served.reshape(2, count, capacity, KT, heads_here, head_dim),
        "tok",
        split_axis=1,
        concat_axis=1,
        tiled=True,
    )
    fetched = fetched.reshape(2, slots, KT, heads_here, head_dim)
    far_pair = jnp.take(fetched, position, axis=1).reshape(2, ncrit * KT, heads_here, head_dim)
    window = padded(pair, (("tok", 1),), KT)
    key_pair = jnp.concatenate([window, far_pair], axis=1)
    valid = jnp.concatenate(
        [
            jnp.broadcast_to(has_left, (KT,)),
            jnp.ones((tok_rows,), bool),
            jnp.broadcast_to(has_right, (KT,)),
            jnp.repeat(used, KT),
        ]
    )
    scale = head_dim ** (-0.5)
    key_all = key_pair[0]
    value_all = key_pair[1]
    scores = (
        jnp.einsum("qhd,khd->hqk", queries, key_all, preferred_element_type=jnp.float32) * scale
    )
    scores = jnp.where(valid[None, None, :], scores, -1e30)
    top = jnp.max(scores, axis=-1, keepdims=True)
    probs = jnp.exp(scores - top)
    probs = probs / jnp.sum(probs, axis=-1, keepdims=True)
    probs_b = probs.astype(jnp.bfloat16)
    dprob = jnp.einsum("qhd,khd->hqk", d_attn, value_all, preferred_element_type=jnp.float32)
    delta = jnp.sum(probs * dprob, axis=-1, keepdims=True)
    dscore = (probs * (dprob - delta) * scale).astype(jnp.bfloat16)
    grad_q = jnp.einsum("hqk,khd->qhd", dscore, key_all, preferred_element_type=jnp.float32).astype(
        jnp.bfloat16
    )
    part_k = jnp.einsum("hqk,qhd->khd", dscore, queries, preferred_element_type=jnp.float32)
    part_v = jnp.einsum("hqk,qhd->khd", probs_b, d_attn, preferred_element_type=jnp.float32)
    grads = jnp.stack([part_k, part_v]) * valid.astype(jnp.float32)[None, :, None, None]
    left_part = grads[:, :KT]
    own_part = grads[:, KT : KT + tok_rows]
    right_part = grads[:, KT + tok_rows : 2 * KT + tok_rows]
    far_part = grads[:, 2 * KT + tok_rows :].reshape(2, ncrit, row_len)
    slotted = jnp.einsum(
        "cs,ecr->esr", chosen.astype(jnp.float32), far_part, precision=lax.Precision.HIGHEST
    )
    returned = lax.all_to_all(
        slotted.reshape(2, count, capacity, row_len).astype(jnp.bfloat16),
        "tok",
        split_axis=1,
        concat_axis=1,
        tiled=True,
    ).astype(jnp.float32)
    returned = returned.reshape(2, slots, row_len)
    owned = (asked[None, :] == jnp.arange(tiles_here)[:, None]).astype(jnp.float32)
    added = jnp.einsum("ts,esr->etr", owned, returned, precision=lax.Precision.HIGHEST)
    total = own_part + added.reshape(2, tok_rows, heads_here, head_dim)
    from_next = shifted(left_part.astype(jnp.bfloat16), "tok", -1).astype(left_part.dtype)
    from_prev = shifted(right_part.astype(jnp.bfloat16), "tok", 1).astype(right_part.dtype)
    total = total + jnp.pad(from_next, ((0, 0), (tok_rows - KT, 0), (0, 0), (0, 0)))
    total = total + jnp.pad(from_prev, ((0, 0), (0, tok_rows - KT), (0, 0), (0, 0)))
    return (grad_q, total[0].astype(jnp.bfloat16), total[1].astype(jnp.bfloat16))


def solution(mesh):
    return jax.shard_map(
        shards,
        mesh=mesh,
        in_specs=(
            P("tok", "head", None),
            P("tok", "head", None),
            P("tok", "head", None),
            P("tok", "head"),
            P("head", None),
            P("tok", None),
        ),
        out_specs=(P("tok", "head", None), P("tok", "head", None), P("tok", "head", None)),
        check_vma=False,
    )
```

```python
import functools

import jax
import jax.numpy as jnp
from jax import lax
from jax.experimental import pallas as pl
from jax.experimental.pallas import tpu as pltpu
from jax.sharding import PartitionSpec as P

KT = 16
LANES = 128
MASKED = -1e30
MESH = pl.DeviceIdType.MESH
NT = (((1,), (1,)), ((), ()))


def owner_of(h, group, count, heads):
    gap = count - heads
    spread = jnp.where(h == 0, 0, jnp.where(h == heads - 1, gap, gap // 2))
    return h + jnp.where(group % 2 == 1, spread, gap // 2)


def head_of(me, group, count, heads):
    gap = count - heads
    odd = group % 2 == 1
    head = me - gap // 2
    inner = jnp.where(odd, 1, 0)
    owns = (head >= inner) & (head < heads - inner)
    head = jnp.where(odd & (me == 0), 0, jnp.where(odd & (me == count - 1), heads - 1, head))
    owns = owns | (odd & ((me == 0) | (me == count - 1)))
    return jnp.clip(head, 0, heads - 1), owns


def by_head_kernel(
    count, groups, ncrit, crit, q_in, k_in, v_in, go_in, w_in, grads,
    q_all, k_all, v_all, d_all, info_own, info_all, info, go_all, w_all, acc, d_own, onehot, k_sel,
    k_turned, v_sel, weights, scores, dprob, inverse, dk_part, dv_part, dq_st, dk_st, dv_st,
    info_sem, send_in, recv_in, send_go, recv_go, w_sem, send_out, recv_out,
):
    heads, rows, dim = q_in.shape
    tiles_here = rows // KT
    width = go_in.shape[1]
    me = lax.axis_index("tok")
    group = lax.axis_index("head")
    head, owns = head_of(me, group, count, heads)

    barrier = pltpu.get_barrier_semaphore()
    for step in range(1, count):
        pl.semaphore_signal(
            barrier, inc=1, device_id=((me + step) % count, group), device_id_type=MESH
        )
    mate = group + 1 - 2 * (group % 2)
    across = (group + groups // 2) % groups
    for other in (mate, across):
        pl.semaphore_signal(barrier, inc=1, device_id=(me, other), device_id_type=MESH)
    loads = []
    for s in range(groups):
        load = pltpu.make_async_copy(w_in.at[:, pl.ds(s * width, width)], w_all.at[s], w_sem.at[s])
        load.start()
        loads.append(load)
    near = tiles_here + 2
    slots = weights.shape[1] // KT
    chunks = weights.shape[1] // rows
    lane = lax.broadcasted_iota(jnp.int32, (8, LANES), 1)
    first = me * tiles_here - 1
    tile_in = first + lane
    tile_in = jnp.where((lane < near) & (tile_in >= 0) & (tile_in < count * tiles_here), tile_in, -1)
    slot_of = jnp.where((lane >= first) & (lane < first + near), lane - first, slots - 1)
    for c in range(ncrit):
        tile_in = jnp.where(lane == near + c, crit[0, c], tile_in)
        slot_of = jnp.where(lane == crit[0, c], near + c, slot_of)
    row = lax.broadcasted_iota(jnp.int32, (8, LANES), 0)
    info_own[...] = jnp.where(row == 0, jnp.maximum(tile_in, 0), jnp.where(row == 1, slot_of, tile_in))
    pl.semaphore_wait(barrier, count - 1 + 2)

    def go_copy(step):
        to = across if step == 2 else mate
        shard = across if step == 3 else group
        return pltpu.make_async_remote_copy(
            src_ref=go_all.at[across] if step == 3 else go_in,
            dst_ref=go_all.at[shard],
            send_sem=send_go.at[step],
            recv_sem=recv_go.at[step],
            device_id=(me, to),
            device_id_type=MESH,
        )

    go_copy(2).start()
    go_copy(1).start()
    own_go = pltpu.make_async_copy(go_in, go_all.at[group], recv_go.at[0])
    own_go.start()

    here = pl.ds(pl.multiple_of(me * rows, rows), rows)
    own_tiles = pl.ds(me * tiles_here, tiles_here)

    def target(i):
        half = heads // 2
        far = jnp.where(me < count // 2, half, 0)
        h = (far + (i % half + me) % half + (i // half) * half) % heads
        return h, owner_of(h, group, count, heads)

    def in_copy(kind, src, dst, h, owner):
        return pltpu.make_async_remote_copy(
            src_ref=src,
            dst_ref=dst,
            send_sem=send_in.at[kind, h],
            recv_sem=recv_in.at[kind, me],
            device_id=(owner, group),
            device_id_type=MESH,
        )

    def send(kind, src, dst, h, owner):
        @pl.when(owner != me)
        def _():
            in_copy(kind, src, dst, h, owner).start()

        @pl.when(owner == me)
        def _():
            pltpu.make_async_copy(src, dst, recv_in.at[kind, me]).start()

    for i in range(heads):
        h, owner = target(i)
        send(4, info_own, info_all.at[me], h, owner)
        send(0, k_in.at[h], k_all.at[own_tiles], h, owner)
    for i in range(heads):
        h, owner = target(i)
        send(1, q_in.at[h], q_all.at[here], h, owner)
    for i in range(heads):
        h, owner = target(i)
        send(2, v_in.at[h], v_all.at[own_tiles], h, owner)

    for step in range(groups):
        src = (group, mate, across, (mate + groups // 2) % groups)[step]
        if step == 0:
            own_go.wait()
        else:
            go_copy(step).wait_recv()
        if step == 2:
            go_copy(3).start()
        if step == 0:
            for load in loads:
                load.wait()
        part = lax.dot_general(
            go_all[src], w_all[src], NT, preferred_element_type=jnp.float32
        )
        if step == 0:
            acc[...] = part
        elif step < groups - 1:
            acc[...] += part
        else:
            done = (acc[...] + part).astype(jnp.bfloat16)
            for h in range(heads):
                d_own[h] = done[:, h * dim : (h + 1) * dim]
    for i in range(heads):
        h, owner = target(i)
        send(3, d_own.at[h], d_all.at[here], h, owner)

    def landed(kind, dst, b):
        in_copy_from = pltpu.make_async_remote_copy(
            src_ref=dst,
            dst_ref=dst,
            send_sem=send_in.at[kind, 0],
            recv_sem=recv_in.at[kind, b],
            device_id=((me + 1) % count, group),
            device_id_type=MESH,
        )
        in_copy_from.wait_recv()

    def block(b):
        return pl.ds(pl.multiple_of(b * rows, rows), rows)

    def tiles_of(b):
        return pl.ds(b * tiles_here, tiles_here)

    scale = dim ** (-0.5)
    low = me < count // 2

    def near_first(i):
        b = jnp.where(low, i, count - 1 - i)
        return b + ((me + group) % 2) * (1 - 2 * (b % 2))

    @pl.when(owns)
    def _():
        def arrived(b, carry):
            landed(4, info_all.at[b], b)
            landed(0, k_all.at[tiles_of(b)], b)
            return carry

        lax.fori_loop(0, count, arrived, 0)
        to_scalars = pltpu.make_async_copy(info_all, info, info_sem)
        to_scalars.start()
        to_scalars.wait()

        def pick(source, chosen, b):
            for s in range(slots):
                chosen[b, s * KT : (s + 1) * KT, :] = source[info[b, 0, s]]

        def prepare(b, carry):
            pick(k_all, k_sel, b)
            for j in range(chunks):
                at = slice(j * rows, (j + 1) * rows)
                k_turned[b, j] = k_sel[b, at, :].T
            return carry

        lax.fori_loop(0, count, prepare, 0)
        for j in range(chunks):
            slot_id = lax.broadcasted_iota(jnp.int32, (rows, LANES), 1)
            of_row = j * (rows // KT) + lax.broadcasted_iota(jnp.int32, (rows, LANES), 0) // KT
            onehot[j * rows : (j + 1) * rows, :] = jnp.where(slot_id == of_row, 1.0, 0.0).astype(
                jnp.bfloat16
            )

        def forward(i, carry):
            b = near_first(i)
            landed(1, q_all.at[block(b)], b)
            bias = jnp.where(info_all[b][2:3, :] >= 0, 0.0, MASKED)
            bias = jnp.broadcast_to(bias, (rows, LANES)).astype(jnp.bfloat16)
            query = jnp.concatenate([q_all[block(b), :], bias], axis=1)
            top = jnp.full((8, rows), MASKED, jnp.float32)
            for j in range(chunks):
                at = slice(j * rows, (j + 1) * rows)
                key = jnp.concatenate([k_sel[b, at, :], onehot[at, :]], axis=1)
                s = lax.dot_general(key, query, NT, preferred_element_type=jnp.float32)
                scores[at, :] = s
                top = jnp.maximum(top, jnp.max(s.reshape(rows // 8, 8, rows), axis=0))
            top = jnp.max(top, axis=0, keepdims=True)
            factor = scale * 1.4426950408889634
            summed = jnp.zeros((8, rows), jnp.float32)
            for j in range(chunks):
                at = slice(j * rows, (j + 1) * rows)
                e = jnp.exp2((scores[at, :] - top) * factor)
                weights[b, at, :] = e.astype(jnp.bfloat16)
                summed = summed + jnp.sum(e.reshape(rows // 8, 8, rows), axis=0)
            inv = 1.0 / jnp.sum(summed, axis=0, keepdims=True)
            inverse[b] = jnp.broadcast_to(inv, (8, rows))
            return carry

        lax.fori_loop(0, count, forward, 0)

        def values_in(b, carry):
            landed(2, v_all.at[tiles_of(b)], b)
            return carry

        lax.fori_loop(0, count, values_in, 0)

        def pick_values(b, carry):
            pick(v_all, v_sel, b)
            return carry

        lax.fori_loop(0, count, pick_values, 0)

        def backward(i, carry):
            b = near_first(i)
            landed(3, d_all.at[block(b)], b)
            d_b = d_all[block(b), :]
            q_b = q_all[block(b), :]
            inv = inverse[b][0:1, :]
            delta = jnp.zeros((8, rows), jnp.float32)
            for j in range(chunks):
                at = slice(j * rows, (j + 1) * rows)
                dp = lax.dot_general(v_sel[b, at, :], d_b, NT, preferred_element_type=jnp.float32)
                dprob[at, :] = dp
                w = weights[b, at, :].astype(jnp.float32) * dp
                delta = delta + jnp.sum(w.reshape(rows // 8, 8, rows), axis=0)
            delta = jnp.sum(delta, axis=0, keepdims=True) * inv
            dq = jnp.zeros((dim, rows), jnp.float32)
            for j in range(chunks):
                at = slice(j * rows, (j + 1) * rows)
                p = weights[b, at, :].astype(jnp.float32) * inv
                ds = (p * (dprob[at, :] - delta)).astype(jnp.bfloat16)
                dv = jnp.dot(p.astype(jnp.bfloat16), d_b, preferred_element_type=jnp.float32)
                dk = jnp.dot(ds, q_b, preferred_element_type=jnp.float32)
                part = slice(j * tiles_here, (j + 1) * tiles_here)
                dv_part[b, part] = dv.reshape(tiles_here, KT, dim)
                dk_part[b, part] = dk.reshape(tiles_here, KT, dim)
                dq = dq + jnp.dot(k_turned[b, j], ds, preferred_element_type=jnp.float32)
            dq_st[block(b), :] = (dq * scale).T.astype(jnp.bfloat16)
            give(0, dq_st, b)
            return carry

        def out_copy(kind, staged, b):
            return pltpu.make_async_remote_copy(
                src_ref=staged.at[block(b)],
                dst_ref=grads.at[kind, head],
                send_sem=send_out.at[kind, b],
                recv_sem=recv_out.at[kind, head],
                device_id=(b, group),
                device_id_type=MESH,
            )

        def give(kind, staged, b):
            @pl.when(b != me)
            def _():
                out_copy(kind, staged, b).start()

            @pl.when(b == me)
            def _():
                pltpu.make_async_copy(
                    staged.at[block(b)], grads.at[kind, head], recv_out.at[kind, head]
                ).start()

        lax.fori_loop(0, count, backward, 0)

        def finish(i, carry):
            b = near_first(count - 1 - i)
            for t in range(tiles_here):
                dk = jnp.zeros((KT, dim), jnp.float32)
                dv = jnp.zeros((KT, dim), jnp.float32)
                for c in range(count):
                    slot = info[c, 1, b * tiles_here + t]
                    dk = dk + dk_part[c, slot]
                    dv = dv + dv_part[c, slot]
                at = pl.ds(pl.multiple_of(b * rows + t * KT, KT), KT)
                dk_st[at, :] = (dk * scale).astype(jnp.bfloat16)
                dv_st[at, :] = dv.astype(jnp.bfloat16)
            give(1, dk_st, b)
            give(2, dv_st, b)
            return carry

        lax.fori_loop(0, count, finish, 0)

        def sent(b, carry):
            @pl.when(b != me)
            def _():
                for kind, staged in ((0, dq_st), (1, dk_st), (2, dv_st)):
                    out_copy(kind, staged, b).wait_send()

            return carry

        lax.fori_loop(0, count, sent, 0)

    for step in range(1, groups):
        go_copy(step).wait_send()
    for h in range(heads):
        owner = owner_of(h, group, count, heads)

        @pl.when(owner != me)
        def _():
            in_copy(0, k_in.at[h], k_all.at[own_tiles], h, owner).wait_send()
            in_copy(1, q_in.at[h], q_all.at[here], h, owner).wait_send()
            in_copy(2, v_in.at[h], v_all.at[own_tiles], h, owner).wait_send()
            in_copy(3, d_own.at[h], d_all.at[here], h, owner).wait_send()
            in_copy(4, info_own, info_all.at[me], h, owner).wait_send()

        for kind in range(3):
            pltpu.make_async_remote_copy(
                src_ref=grads.at[kind, h],
                dst_ref=grads.at[kind, h],
                send_sem=send_out.at[kind, 0],
                recv_sem=recv_out.at[kind, h],
                device_id=((me + 1) % count, group),
                device_id_type=MESH,
            ).wait_recv()


def by_head(queries, keys, values, grad_out, w_out, crit):
    rows, heads, dim = queries.shape
    count = lax.axis_size("tok")
    groups = lax.axis_size("head")
    total = count * rows
    width = grad_out.shape[1]
    tiles_here = rows // KT
    chosen = ((tiles_here + 2 + crit.shape[1]) // tiles_here + 1) * rows
    bf16, f32 = jnp.bfloat16, jnp.float32
    hbm = pl.BlockSpec(memory_space=pl.ANY)
    vmem, dma = pltpu.VMEM, pltpu.SemaphoreType.DMA
    out = jax.ShapeDtypeStruct((3, heads, rows, dim), bf16)
    grads = pl.pallas_call(
        functools.partial(by_head_kernel, count, groups, crit.shape[1]),
        out_shape=out,
        in_specs=[pl.BlockSpec(memory_space=pltpu.SMEM)] + [hbm] * 5,
        out_specs=hbm,
        scratch_shapes=[
            vmem((total, dim), bf16),
            vmem((total // KT, KT, dim), bf16),
            vmem((total // KT, KT, dim), bf16),
            vmem((total, dim), bf16),
            vmem((8, LANES), jnp.int32),
            vmem((count, 8, LANES), jnp.int32),
            pltpu.SMEM((count, 8, LANES), jnp.int32),
            vmem((groups, rows, width), bf16),
            vmem((groups, w_out.shape[0], width), bf16),
            vmem((rows, heads * dim), f32),
            vmem((heads, rows, dim), bf16),
            vmem((chosen, LANES), bf16),
            vmem((count, chosen, dim), bf16),
            vmem((count, chosen // rows, dim, rows), bf16),
            vmem((count, chosen, dim), bf16),
            vmem((count, chosen, rows), bf16),
            vmem((chosen, rows), f32),
            vmem((chosen, rows), f32),
            vmem((count, 8, rows), f32),
            vmem((count, chosen // KT, KT, dim), f32),
            vmem((count, chosen // KT, KT, dim), f32),
            vmem((total, dim), bf16),
            vmem((total, dim), bf16),
            vmem((total, dim), bf16),
            dma,
            dma((5, heads)),
            dma((5, count)),
            dma((groups,)),
            dma((groups,)),
            dma((groups,)),
            dma((3, count)),
            dma((3, heads)),
        ],
        compiler_params=pltpu.CompilerParams(
            collective_id=0, has_side_effects=True, vmem_limit_bytes=63 * 2**20 + 2**19
        ),
    )(
        crit,
        jnp.transpose(queries, (1, 0, 2)),
        jnp.transpose(keys, (1, 0, 2)).reshape(heads, tiles_here, KT, dim),
        jnp.transpose(values, (1, 0, 2)).reshape(heads, tiles_here, KT, dim),
        grad_out,
        w_out,
    )
    return tuple(jnp.transpose(grads[kind], (1, 0, 2)) for kind in range(3))


def padded(cells, sides, width):
    for axis, dim in sides:
        count = lax.axis_size(axis)
        ends = count - 1
        head = lax.slice_in_dim(cells, 0, width, axis=dim)
        tail = lax.slice_in_dim(cells, cells.shape[dim] - width, cells.shape[dim], axis=dim)
        cells = jnp.concatenate(
            [
                lax.ppermute(tail, axis, [(i, (i + 1) % count) for i in range(ends)]),
                cells,
                lax.ppermute(head, axis, [((i + 1) % count, i) for i in range(ends)]),
            ],
            axis=dim,
        )
    return cells


def shifted(value, axis, steps):
    count = lax.axis_size(axis)
    leading, last = (max(0, -steps), min(count, count - steps))
    return lax.ppermute(value, axis, [(source, source + steps) for source in range(leading, last)])


def shards(queries, keys, values, grad_out, w_out, crit):
    tok_rows, heads_here, head_dim = queries.shape
    width_here = heads_here * head_dim
    count = lax.axis_size("tok")
    place = lax.axis_index("tok")
    tiles_here = tok_rows // KT
    if lax.axis_size("head") == 4 and count % 2 == 0 and 2 < heads_here <= count <= 2 * heads_here and count * tiles_here <= LANES and tok_rows % KT == 0 and tiles_here + crit.shape[1] < 110:
        return by_head(queries, keys, values, grad_out, w_out, crit)
    ncrit = crit.shape[1]
    capacity = (ncrit + count - 4) // (count - 3)
    slots = count * capacity
    row_len = KT * width_here
    d_attn = lax.dot_general(
        lax.all_gather(grad_out, "head", axis=1, tiled=True),
        w_out,
        (((1,), (1,)), ((), ())),
        preferred_element_type=jnp.float32,
    )
    d_attn = d_attn.astype(jnp.bfloat16).reshape(tok_rows, heads_here, head_dim)
    tiles = crit[0]
    used = tiles >= 0
    owner = jnp.where(used, tiles // tiles_here, -1)
    local_tile = jnp.where(used, tiles % tiles_here, 0)
    order = jnp.arange(ncrit)
    earlier = (owner[:, None] == owner[None, :]) & (order[:, None] > order[None, :]) & used[None, :]
    slot = jnp.sum(earlier.astype(jnp.int32), axis=1)
    position = jnp.where(used, owner * capacity + slot, 0)
    slot_ids = jnp.arange(slots)
    chosen = used[:, None] & (position[:, None] == slot_ids[None, :])
    request = jnp.sum(jnp.where(chosen, local_tile[:, None] + 1, 0), axis=0) - 1
    has_left = place > 0
    has_right = place < count - 1
    asked = lax.all_to_all(
        request.reshape(count, capacity), "tok", split_axis=0, concat_axis=0, tiled=True
    ).reshape(slots)
    pair = jnp.stack([keys, values])
    pair_tiles = pair.reshape(2, tiles_here, KT, heads_here, head_dim)
    served = jnp.take(pair_tiles, jnp.clip(asked, 0, tiles_here - 1), axis=1)
    served = jnp.where((asked >= 0)[None, :, None, None, None], served, jnp.zeros((), jnp.bfloat16))
    fetched = lax.all_to_all(
        served.reshape(2, count, capacity, KT, heads_here, head_dim),
        "tok",
        split_axis=1,
        concat_axis=1,
        tiled=True,
    )
    fetched = fetched.reshape(2, slots, KT, heads_here, head_dim)
    far_pair = jnp.take(fetched, position, axis=1).reshape(2, ncrit * KT, heads_here, head_dim)
    window = padded(pair, (("tok", 1),), KT)
    key_pair = jnp.concatenate([window, far_pair], axis=1)
    valid = jnp.concatenate(
        [
            jnp.broadcast_to(has_left, (KT,)),
            jnp.ones((tok_rows,), bool),
            jnp.broadcast_to(has_right, (KT,)),
            jnp.repeat(used, KT),
        ]
    )
    scale = head_dim ** (-0.5)
    key_all = key_pair[0]
    value_all = key_pair[1]
    scores = (
        jnp.einsum("qhd,khd->hqk", queries, key_all, preferred_element_type=jnp.float32) * scale
    )
    scores = jnp.where(valid[None, None, :], scores, -1e30)
    top = jnp.max(scores, axis=-1, keepdims=True)
    probs = jnp.exp(scores - top)
    probs = probs / jnp.sum(probs, axis=-1, keepdims=True)
    probs_b = probs.astype(jnp.bfloat16)
    dprob = jnp.einsum("qhd,khd->hqk", d_attn, value_all, preferred_element_type=jnp.float32)
    delta = jnp.sum(probs * dprob, axis=-1, keepdims=True)
    dscore = (probs * (dprob - delta) * scale).astype(jnp.bfloat16)
    grad_q = jnp.einsum("hqk,khd->qhd", dscore, key_all, preferred_element_type=jnp.float32).astype(
        jnp.bfloat16
    )
    part_k = jnp.einsum("hqk,qhd->khd", dscore, queries, preferred_element_type=jnp.float32)
    part_v = jnp.einsum("hqk,qhd->khd", probs_b, d_attn, preferred_element_type=jnp.float32)
    grads = jnp.stack([part_k, part_v]) * valid.astype(jnp.float32)[None, :, None, None]
    left_part = grads[:, :KT]
    own_part = grads[:, KT : KT + tok_rows]
    right_part = grads[:, KT + tok_rows : 2 * KT + tok_rows]
    far_part = grads[:, 2 * KT + tok_rows :].reshape(2, ncrit, row_len)
    slotted = jnp.einsum(
        "cs,ecr->esr", chosen.astype(jnp.float32), far_part, precision=lax.Precision.HIGHEST
    )
    returned = lax.all_to_all(
        slotted.reshape(2, count, capacity, row_len).astype(jnp.bfloat16),
        "tok",
        split_axis=1,
        concat_axis=1,
        tiled=True,
    ).astype(jnp.float32)
    returned = returned.reshape(2, slots, row_len)
    owned = (asked[None, :] == jnp.arange(tiles_here)[:, None]).astype(jnp.float32)
    added = jnp.einsum("ts,esr->etr", owned, returned, precision=lax.Precision.HIGHEST)
    total = own_part + added.reshape(2, tok_rows, heads_here, head_dim)
    from_next = shifted(left_part.astype(jnp.bfloat16), "tok", -1).astype(left_part.dtype)
    from_prev = shifted(right_part.astype(jnp.bfloat16), "tok", 1).astype(right_part.dtype)
    total = total + jnp.pad(from_next, ((0, 0), (tok_rows - KT, 0), (0, 0), (0, 0)))
    total = total + jnp.pad(from_prev, ((0, 0), (0, tok_rows - KT), (0, 0), (0, 0)))
    return (grad_q, total[0].astype(jnp.bfloat16), total[1].astype(jnp.bfloat16))


def solution(mesh):
    return jax.shard_map(
        shards,
        mesh=mesh,
        in_specs=(
            P("tok", "head", None),
            P("tok", "head", None),
            P("tok", "head", None),
            P("tok", "head"),
            P("head", None),
            P("tok", None),
        ),
        out_specs=(P("tok", "head", None), P("tok", "head", None), P("tok", "head", None)),
        check_vma=False,
    )
```

```python
import functools

import jax
import jax.numpy as jnp
from jax import lax
from jax.experimental import pallas as pl
from jax.experimental.pallas import tpu as pltpu
from jax.sharding import PartitionSpec as P

KT = 16
LANES = 128
MASKED = -1e30
MESH = pl.DeviceIdType.MESH
NT = (((1,), (1,)), ((), ()))


def owner_of(h, group, count, heads):
    gap = count - heads
    spread = jnp.where(h == 0, 0, jnp.where(h == heads - 1, gap, gap // 2))
    return h + jnp.where(group % 2 == 1, spread, gap // 2)


def head_of(me, group, count, heads):
    gap = count - heads
    odd = group % 2 == 1
    head = me - gap // 2
    inner = jnp.where(odd, 1, 0)
    owns = (head >= inner) & (head < heads - inner)
    head = jnp.where(odd & (me == 0), 0, jnp.where(odd & (me == count - 1), heads - 1, head))
    owns = owns | (odd & ((me == 0) | (me == count - 1)))
    return jnp.clip(head, 0, heads - 1), owns


def by_head_kernel(
    count, groups, ncrit, crit, q_in, k_in, v_in, go_in, w_in, grads,
    q_all, k_all, v_all, d_all, info_own, info_all, info, go_all, w_all, acc, d_own, onehot, k_sel,
    k_turned, v_sel, weights, scores, dprob, inverse, dk_part, dv_part, dq_st, dk_st, dv_st,
    info_sem, send_in, recv_in, send_go, recv_go, w_sem, send_out, recv_out,
):
    heads, rows, dim = q_in.shape
    tiles_here = rows // KT
    width = go_in.shape[1]
    me = lax.axis_index("tok")
    group = lax.axis_index("head")
    head, owns = head_of(me, group, count, heads)

    barrier = pltpu.get_barrier_semaphore()
    for step in range(1, count):
        pl.semaphore_signal(
            barrier, inc=1, device_id=((me + step) % count, group), device_id_type=MESH
        )
    mate = group + 1 - 2 * (group % 2)
    across = (group + groups // 2) % groups
    for other in (mate, across):
        pl.semaphore_signal(barrier, inc=1, device_id=(me, other), device_id_type=MESH)
    loads = []
    for s in range(groups):
        load = pltpu.make_async_copy(w_in.at[:, pl.ds(s * width, width)], w_all.at[s], w_sem.at[s])
        load.start()
        loads.append(load)
    near = tiles_here + 2
    slots = weights.shape[1] // KT
    chunks = weights.shape[1] // rows
    lane = lax.broadcasted_iota(jnp.int32, (8, LANES), 1)
    first = me * tiles_here - 1
    tile_in = first + lane
    tile_in = jnp.where((lane < near) & (tile_in >= 0) & (tile_in < count * tiles_here), tile_in, -1)
    slot_of = jnp.where((lane >= first) & (lane < first + near), lane - first, slots - 1)
    for c in range(ncrit):
        tile_in = jnp.where(lane == near + c, crit[0, c], tile_in)
        slot_of = jnp.where(lane == crit[0, c], near + c, slot_of)
    row = lax.broadcasted_iota(jnp.int32, (8, LANES), 0)
    info_own[...] = jnp.where(row == 0, jnp.maximum(tile_in, 0), jnp.where(row == 1, slot_of, tile_in))
    pl.semaphore_wait(barrier, count - 1 + 2)

    def go_copy(step):
        to = across if step == 2 else mate
        shard = across if step == 3 else group
        return pltpu.make_async_remote_copy(
            src_ref=go_all.at[across] if step == 3 else go_in,
            dst_ref=go_all.at[shard],
            send_sem=send_go.at[step],
            recv_sem=recv_go.at[step],
            device_id=(me, to),
            device_id_type=MESH,
        )

    go_copy(2).start()
    go_copy(1).start()
    own_go = pltpu.make_async_copy(go_in, go_all.at[group], recv_go.at[0])
    own_go.start()

    here = pl.ds(pl.multiple_of(me * rows, rows), rows)
    own_tiles = pl.ds(me * tiles_here, tiles_here)

    def target(i):
        half = heads // 2
        far = jnp.where(me < count // 2, half, 0)
        h = (far + (i % half + me) % half + (i // half) * half) % heads
        return h, owner_of(h, group, count, heads)

    def in_copy(kind, src, dst, h, owner):
        return pltpu.make_async_remote_copy(
            src_ref=src,
            dst_ref=dst,
            send_sem=send_in.at[kind, h],
            recv_sem=recv_in.at[kind, me],
            device_id=(owner, group),
            device_id_type=MESH,
        )

    def send(kind, src, dst, h, owner):
        @pl.when(owner != me)
        def _():
            in_copy(kind, src, dst, h, owner).start()

        @pl.when(owner == me)
        def _():
            pltpu.make_async_copy(src, dst, recv_in.at[kind, me]).start()

    for i in range(heads):
        h, owner = target(i)
        send(4, info_own, info_all.at[me], h, owner)
        send(0, k_in.at[h], k_all.at[own_tiles], h, owner)
    for i in range(heads):
        h, owner = target(i)
        send(1, q_in.at[h], q_all.at[here], h, owner)
    for i in range(heads):
        h, owner = target(i)
        send(2, v_in.at[h], v_all.at[own_tiles], h, owner)

    for step in range(groups):
        src = (group, mate, across, (mate + groups // 2) % groups)[step]
        if step == 0:
            own_go.wait()
        else:
            go_copy(step).wait_recv()
        if step == 2:
            go_copy(3).start()
        if step == 0:
            for load in loads:
                load.wait()
        part = lax.dot_general(
            go_all[src], w_all[src], NT, preferred_element_type=jnp.float32
        )
        if step == 0:
            acc[...] = part
        elif step < groups - 1:
            acc[...] += part
        else:
            done = (acc[...] + part).astype(jnp.bfloat16)
            for h in range(heads):
                d_own[h] = done[:, h * dim : (h + 1) * dim]
    for i in range(heads):
        h, owner = target(i)
        send(3, d_own.at[h], d_all.at[here], h, owner)

    def landed(kind, dst, b):
        in_copy_from = pltpu.make_async_remote_copy(
            src_ref=dst,
            dst_ref=dst,
            send_sem=send_in.at[kind, 0],
            recv_sem=recv_in.at[kind, b],
            device_id=((me + 1) % count, group),
            device_id_type=MESH,
        )
        in_copy_from.wait_recv()

    def block(b):
        return pl.ds(pl.multiple_of(b * rows, rows), rows)

    def tiles_of(b):
        return pl.ds(b * tiles_here, tiles_here)

    scale = dim ** (-0.5)
    low = me < count // 2

    def near_first(i):
        b = jnp.where(low, i, count - 1 - i)
        return b + ((me + group) % 2) * (1 - 2 * (b % 2))

    @pl.when(owns)
    def _():
        def arrived(b, carry):
            landed(4, info_all.at[b], b)
            landed(0, k_all.at[tiles_of(b)], b)
            return carry

        lax.fori_loop(0, count, arrived, 0)
        to_scalars = pltpu.make_async_copy(info_all, info, info_sem)
        to_scalars.start()
        to_scalars.wait()

        def pick(source, chosen, b):
            for s in range(slots):
                chosen[b, s * KT : (s + 1) * KT, :] = source[info[b, 0, s]]

        def prepare(b, carry):
            pick(k_all, k_sel, b)
            for j in range(chunks):
                at = slice(j * rows, (j + 1) * rows)
                k_turned[b, j] = k_sel[b, at, :].T
            return carry

        lax.fori_loop(0, count, prepare, 0)
        for j in range(chunks):
            slot_id = lax.broadcasted_iota(jnp.int32, (rows, LANES), 1)
            of_row = j * (rows // KT) + lax.broadcasted_iota(jnp.int32, (rows, LANES), 0) // KT
            onehot[j * rows : (j + 1) * rows, :] = jnp.where(slot_id == of_row, 1.0, 0.0).astype(
                jnp.bfloat16
            )

        def forward(i, carry):
            b = near_first(i)
            landed(1, q_all.at[block(b)], b)
            bias = jnp.where(info_all[b][2:3, :] >= 0, 0.0, MASKED)
            bias = jnp.broadcast_to(bias, (rows, LANES)).astype(jnp.bfloat16)
            query = jnp.concatenate([q_all[block(b), :], bias], axis=1)
            top = jnp.full((8, rows), MASKED, jnp.float32)
            for j in range(chunks):
                at = slice(j * rows, (j + 1) * rows)
                key = jnp.concatenate([k_sel[b, at, :], onehot[at, :]], axis=1)
                s = lax.dot_general(key, query, NT, preferred_element_type=jnp.float32)
                scores[at, :] = s
                top = jnp.maximum(top, jnp.max(s.reshape(rows // 8, 8, rows), axis=0))
            top = jnp.max(top, axis=0, keepdims=True)
            factor = scale * 1.4426950408889634
            summed = jnp.zeros((8, rows), jnp.float32)
            for j in range(chunks):
                at = slice(j * rows, (j + 1) * rows)
                e = jnp.exp2((scores[at, :] - top) * factor)
                weights[b, at, :] = e.astype(jnp.bfloat16)
                summed = summed + jnp.sum(e.reshape(rows // 8, 8, rows), axis=0)
            inv = 1.0 / jnp.sum(summed, axis=0, keepdims=True)
            inverse[b] = jnp.broadcast_to(inv, (8, rows))
            return carry

        lax.fori_loop(0, count, forward, 0)

        def values_in(b, carry):
            landed(2, v_all.at[tiles_of(b)], b)
            return carry

        lax.fori_loop(0, count, values_in, 0)

        def pick_values(b, carry):
            pick(v_all, v_sel, b)
            return carry

        lax.fori_loop(0, count, pick_values, 0)

        def backward(i, carry):
            b = near_first((i + count // 2) % count)
            landed(3, d_all.at[block(b)], b)
            d_b = d_all[block(b), :]
            q_b = q_all[block(b), :]
            inv = inverse[b][0:1, :]
            delta = jnp.zeros((8, rows), jnp.float32)
            for j in range(chunks):
                at = slice(j * rows, (j + 1) * rows)
                dp = lax.dot_general(v_sel[b, at, :], d_b, NT, preferred_element_type=jnp.float32)
                dprob[at, :] = dp
                w = weights[b, at, :].astype(jnp.float32) * dp
                delta = delta + jnp.sum(w.reshape(rows // 8, 8, rows), axis=0)
            delta = jnp.sum(delta, axis=0, keepdims=True) * inv
            dq = jnp.zeros((dim, rows), jnp.float32)
            for j in range(chunks):
                at = slice(j * rows, (j + 1) * rows)
                p = weights[b, at, :].astype(jnp.float32) * inv
                ds = (p * (dprob[at, :] - delta)).astype(jnp.bfloat16)
                dv = jnp.dot(p.astype(jnp.bfloat16), d_b, preferred_element_type=jnp.float32)
                dk = jnp.dot(ds, q_b, preferred_element_type=jnp.float32)
                part = slice(j * tiles_here, (j + 1) * tiles_here)
                dv_part[b, part] = dv.reshape(tiles_here, KT, dim)
                dk_part[b, part] = dk.reshape(tiles_here, KT, dim)
                dq = dq + jnp.dot(k_turned[b, j], ds, preferred_element_type=jnp.float32)
            dq_st[block(b), :] = (dq * scale).T.astype(jnp.bfloat16)
            give(0, dq_st, b)
            return carry

        def out_copy(kind, staged, b):
            return pltpu.make_async_remote_copy(
                src_ref=staged.at[block(b)],
                dst_ref=grads.at[kind, head],
                send_sem=send_out.at[kind, b],
                recv_sem=recv_out.at[kind, head],
                device_id=(b, group),
                device_id_type=MESH,
            )

        def give(kind, staged, b):
            @pl.when(b != me)
            def _():
                out_copy(kind, staged, b).start()

            @pl.when(b == me)
            def _():
                pltpu.make_async_copy(
                    staged.at[block(b)], grads.at[kind, head], recv_out.at[kind, head]
                ).start()

        lax.fori_loop(0, count, backward, 0)

        def finish(i, carry):
            b = near_first(count - 1 - i)
            for t in range(tiles_here):
                dk = jnp.zeros((KT, dim), jnp.float32)
                dv = jnp.zeros((KT, dim), jnp.float32)
                for c in range(count):
                    slot = info[c, 1, b * tiles_here + t]
                    dk = dk + dk_part[c, slot]
                    dv = dv + dv_part[c, slot]
                at = pl.ds(pl.multiple_of(b * rows + t * KT, KT), KT)
                dk_st[at, :] = (dk * scale).astype(jnp.bfloat16)
                dv_st[at, :] = dv.astype(jnp.bfloat16)
            give(1, dk_st, b)
            give(2, dv_st, b)
            return carry

        lax.fori_loop(0, count, finish, 0)

        def sent(b, carry):
            @pl.when(b != me)
            def _():
                for kind, staged in ((0, dq_st), (1, dk_st), (2, dv_st)):
                    out_copy(kind, staged, b).wait_send()

            return carry

        lax.fori_loop(0, count, sent, 0)

    for step in range(1, groups):
        go_copy(step).wait_send()
    for h in range(heads):
        owner = owner_of(h, group, count, heads)

        @pl.when(owner != me)
        def _():
            in_copy(0, k_in.at[h], k_all.at[own_tiles], h, owner).wait_send()
            in_copy(1, q_in.at[h], q_all.at[here], h, owner).wait_send()
            in_copy(2, v_in.at[h], v_all.at[own_tiles], h, owner).wait_send()
            in_copy(3, d_own.at[h], d_all.at[here], h, owner).wait_send()
            in_copy(4, info_own, info_all.at[me], h, owner).wait_send()

        for kind in range(3):
            pltpu.make_async_remote_copy(
                src_ref=grads.at[kind, h],
                dst_ref=grads.at[kind, h],
                send_sem=send_out.at[kind, 0],
                recv_sem=recv_out.at[kind, h],
                device_id=((me + 1) % count, group),
                device_id_type=MESH,
            ).wait_recv()


def by_head(queries, keys, values, grad_out, w_out, crit):
    rows, heads, dim = queries.shape
    count = lax.axis_size("tok")
    groups = lax.axis_size("head")
    total = count * rows
    width = grad_out.shape[1]
    tiles_here = rows // KT
    chosen = ((tiles_here + 2 + crit.shape[1]) // tiles_here + 1) * rows
    bf16, f32 = jnp.bfloat16, jnp.float32
    hbm = pl.BlockSpec(memory_space=pl.ANY)
    vmem, dma = pltpu.VMEM, pltpu.SemaphoreType.DMA
    out = jax.ShapeDtypeStruct((3, heads, rows, dim), bf16)
    grads = pl.pallas_call(
        functools.partial(by_head_kernel, count, groups, crit.shape[1]),
        out_shape=out,
        in_specs=[pl.BlockSpec(memory_space=pltpu.SMEM)] + [hbm] * 5,
        out_specs=hbm,
        scratch_shapes=[
            vmem((total, dim), bf16),
            vmem((total // KT, KT, dim), bf16),
            vmem((total // KT, KT, dim), bf16),
            vmem((total, dim), bf16),
            vmem((8, LANES), jnp.int32),
            vmem((count, 8, LANES), jnp.int32),
            pltpu.SMEM((count, 8, LANES), jnp.int32),
            vmem((groups, rows, width), bf16),
            vmem((groups, w_out.shape[0], width), bf16),
            vmem((rows, heads * dim), f32),
            vmem((heads, rows, dim), bf16),
            vmem((chosen, LANES), bf16),
            vmem((count, chosen, dim), bf16),
            vmem((count, chosen // rows, dim, rows), bf16),
            vmem((count, chosen, dim), bf16),
            vmem((count, chosen, rows), bf16),
            vmem((chosen, rows), f32),
            vmem((chosen, rows), f32),
            vmem((count, 8, rows), f32),
            vmem((count, chosen // KT, KT, dim), f32),
            vmem((count, chosen // KT, KT, dim), f32),
            vmem((total, dim), bf16),
            vmem((total, dim), bf16),
            vmem((total, dim), bf16),
            dma,
            dma((5, heads)),
            dma((5, count)),
            dma((groups,)),
            dma((groups,)),
            dma((groups,)),
            dma((3, count)),
            dma((3, heads)),
        ],
        compiler_params=pltpu.CompilerParams(
            collective_id=0, has_side_effects=True, vmem_limit_bytes=63 * 2**20 + 2**19
        ),
    )(
        crit,
        jnp.transpose(queries, (1, 0, 2)),
        jnp.transpose(keys, (1, 0, 2)).reshape(heads, tiles_here, KT, dim),
        jnp.transpose(values, (1, 0, 2)).reshape(heads, tiles_here, KT, dim),
        grad_out,
        w_out,
    )
    return tuple(jnp.transpose(grads[kind], (1, 0, 2)) for kind in range(3))


def padded(cells, sides, width):
    for axis, dim in sides:
        count = lax.axis_size(axis)
        ends = count - 1
        head = lax.slice_in_dim(cells, 0, width, axis=dim)
        tail = lax.slice_in_dim(cells, cells.shape[dim] - width, cells.shape[dim], axis=dim)
        cells = jnp.concatenate(
            [
                lax.ppermute(tail, axis, [(i, (i + 1) % count) for i in range(ends)]),
                cells,
                lax.ppermute(head, axis, [((i + 1) % count, i) for i in range(ends)]),
            ],
            axis=dim,
        )
    return cells


def shifted(value, axis, steps):
    count = lax.axis_size(axis)
    leading, last = (max(0, -steps), min(count, count - steps))
    return lax.ppermute(value, axis, [(source, source + steps) for source in range(leading, last)])


def shards(queries, keys, values, grad_out, w_out, crit):
    tok_rows, heads_here, head_dim = queries.shape
    width_here = heads_here * head_dim
    count = lax.axis_size("tok")
    place = lax.axis_index("tok")
    tiles_here = tok_rows // KT
    if lax.axis_size("head") == 4 and count % 2 == 0 and 2 < heads_here <= count <= 2 * heads_here and count * tiles_here <= LANES and tok_rows % KT == 0 and tiles_here + crit.shape[1] < 110:
        return by_head(queries, keys, values, grad_out, w_out, crit)
    ncrit = crit.shape[1]
    capacity = (ncrit + count - 4) // (count - 3)
    slots = count * capacity
    row_len = KT * width_here
    d_attn = lax.dot_general(
        lax.all_gather(grad_out, "head", axis=1, tiled=True),
        w_out,
        (((1,), (1,)), ((), ())),
        preferred_element_type=jnp.float32,
    )
    d_attn = d_attn.astype(jnp.bfloat16).reshape(tok_rows, heads_here, head_dim)
    tiles = crit[0]
    used = tiles >= 0
    owner = jnp.where(used, tiles // tiles_here, -1)
    local_tile = jnp.where(used, tiles % tiles_here, 0)
    order = jnp.arange(ncrit)
    earlier = (owner[:, None] == owner[None, :]) & (order[:, None] > order[None, :]) & used[None, :]
    slot = jnp.sum(earlier.astype(jnp.int32), axis=1)
    position = jnp.where(used, owner * capacity + slot, 0)
    slot_ids = jnp.arange(slots)
    chosen = used[:, None] & (position[:, None] == slot_ids[None, :])
    request = jnp.sum(jnp.where(chosen, local_tile[:, None] + 1, 0), axis=0) - 1
    has_left = place > 0
    has_right = place < count - 1
    asked = lax.all_to_all(
        request.reshape(count, capacity), "tok", split_axis=0, concat_axis=0, tiled=True
    ).reshape(slots)
    pair = jnp.stack([keys, values])
    pair_tiles = pair.reshape(2, tiles_here, KT, heads_here, head_dim)
    served = jnp.take(pair_tiles, jnp.clip(asked, 0, tiles_here - 1), axis=1)
    served = jnp.where((asked >= 0)[None, :, None, None, None], served, jnp.zeros((), jnp.bfloat16))
    fetched = lax.all_to_all(
        served.reshape(2, count, capacity, KT, heads_here, head_dim),
        "tok",
        split_axis=1,
        concat_axis=1,
        tiled=True,
    )
    fetched = fetched.reshape(2, slots, KT, heads_here, head_dim)
    far_pair = jnp.take(fetched, position, axis=1).reshape(2, ncrit * KT, heads_here, head_dim)
    window = padded(pair, (("tok", 1),), KT)
    key_pair = jnp.concatenate([window, far_pair], axis=1)
    valid = jnp.concatenate(
        [
            jnp.broadcast_to(has_left, (KT,)),
            jnp.ones((tok_rows,), bool),
            jnp.broadcast_to(has_right, (KT,)),
            jnp.repeat(used, KT),
        ]
    )
    scale = head_dim ** (-0.5)
    key_all = key_pair[0]
    value_all = key_pair[1]
    scores = (
        jnp.einsum("qhd,khd->hqk", queries, key_all, preferred_element_type=jnp.float32) * scale
    )
    scores = jnp.where(valid[None, None, :], scores, -1e30)
    top = jnp.max(scores, axis=-1, keepdims=True)
    probs = jnp.exp(scores - top)
    probs = probs / jnp.sum(probs, axis=-1, keepdims=True)
    probs_b = probs.astype(jnp.bfloat16)
    dprob = jnp.einsum("qhd,khd->hqk", d_attn, value_all, preferred_element_type=jnp.float32)
    delta = jnp.sum(probs * dprob, axis=-1, keepdims=True)
    dscore = (probs * (dprob - delta) * scale).astype(jnp.bfloat16)
    grad_q = jnp.einsum("hqk,khd->qhd", dscore, key_all, preferred_element_type=jnp.float32).astype(
        jnp.bfloat16
    )
    part_k = jnp.einsum("hqk,qhd->khd", dscore, queries, preferred_element_type=jnp.float32)
    part_v = jnp.einsum("hqk,qhd->khd", probs_b, d_attn, preferred_element_type=jnp.float32)
    grads = jnp.stack([part_k, part_v]) * valid.astype(jnp.float32)[None, :, None, None]
    left_part = grads[:, :KT]
    own_part = grads[:, KT : KT + tok_rows]
    right_part = grads[:, KT + tok_rows : 2 * KT + tok_rows]
    far_part = grads[:, 2 * KT + tok_rows :].reshape(2, ncrit, row_len)
    slotted = jnp.einsum(
        "cs,ecr->esr", chosen.astype(jnp.float32), far_part, precision=lax.Precision.HIGHEST
    )
    returned = lax.all_to_all(
        slotted.reshape(2, count, capacity, row_len).astype(jnp.bfloat16),
        "tok",
        split_axis=1,
        concat_axis=1,
        tiled=True,
    ).astype(jnp.float32)
    returned = returned.reshape(2, slots, row_len)
    owned = (asked[None, :] == jnp.arange(tiles_here)[:, None]).astype(jnp.float32)
    added = jnp.einsum("ts,esr->etr", owned, returned, precision=lax.Precision.HIGHEST)
    total = own_part + added.reshape(2, tok_rows, heads_here, head_dim)
    from_next = shifted(left_part.astype(jnp.bfloat16), "tok", -1).astype(left_part.dtype)
    from_prev = shifted(right_part.astype(jnp.bfloat16), "tok", 1).astype(right_part.dtype)
    total = total + jnp.pad(from_next, ((0, 0), (tok_rows - KT, 0), (0, 0), (0, 0)))
    total = total + jnp.pad(from_prev, ((0, 0), (0, tok_rows - KT), (0, 0), (0, 0)))
    return (grad_q, total[0].astype(jnp.bfloat16), total[1].astype(jnp.bfloat16))


def solution(mesh):
    return jax.shard_map(
        shards,
        mesh=mesh,
        in_specs=(
            P("tok", "head", None),
            P("tok", "head", None),
            P("tok", "head", None),
            P("tok", "head"),
            P("head", None),
            P("tok", None),
        ),
        out_specs=(P("tok", "head", None), P("tok", "head", None), P("tok", "head", None)),
        check_vma=False,
    )
```
